256 devices in a mesh: expert: 64 (over z_hi, y, x, core), loop: 4 (over z_lo).
Axes of the slice: x: 4, y: 4, z: 8 (z_hi: 2, z_lo: 4; z = z_hi * 4 + z_lo), core: 2. Of those that a mesh axis runs over, the one named last changes fastest.
Arguments:
- tokens: bfloat16 [65536, 1280], P(('expert', 'loop')), may hold values from -6 to 6
- routes: int32 [65536, 1], P(('expert', 'loop')), may hold values from 0 to 63; in each aligned block of 256 rows (0 to 255, 256 to 511, ...) at most 6 rows name the same one
- gate_prob: float32 [65536], P(('expert', 'loop')), may hold values from 0.2 to 1
- expert_quota: int32 [64], replicated, may hold values from 1 to 6, as said below
- w_in: bfloat16 [64, 1280, 5120], P('expert', None, 'loop'), may hold values from -0.15625 to 0.15625
- w_out: bfloat16 [64, 1280, 5120], P('expert', None, 'loop'), may hold values from -0.078125 to 0.078125
- other_pooled: bfloat16 [32512, 1280], P(('expert', 'loop')), may hold values from -6 to 6
- head: bfloat16 [1280, 1024], replicated, may hold values from -0.15625 to 0.15625
- text_embed: bfloat16 [32768, 1024], P(('expert', 'loop')), may hold values from -6 to 6
- labels: int32 [32768], P(('expert', 'loop')), may hold values from 0 to 3
Outputs:
- layer_out: bfloat16 [65536, 1280], P(('expert', 'loop'))
- loss_rows: float32 [32768], P(('expert', 'loop'))
- image_grad: float32 [32768, 1024], P(('expert', 'loop'))
- text_grad: float32 [32768, 1024], P(('expert', 'loop'))
The draws below stay inside these ranges and needn't reach their ends.
Inputs may be any that keep to these rules, and one draw needn't show every extreme that they name: `routes`: in the 256 rows of one device no expert is named by more than 6 rows. `expert_quota`: some expert has a quota of exactly 6.
All inputs are finite; a program needn't handle non-finite values.
Results may differ from the reference program's by a relative error of at most 0.0065.
Values may be sent and summed in bfloat16 or wider, within the bound.
No kernel may reach another device: no remote copies, remote signals or barrier semaphores. Data moves between devices by JAX's collectives and lax.ppermute only.
A program may use at most 128 MiB of HBM per device.

```python
import math
import jax
import jax.numpy as jnp
import numpy as np
from jax import lax

D = 1280
FF = 5120
EMBED = 1024
PATCHES = 256
TOP = 1
PAIRS_DEV = 128
EXPERTS = 64
TOK_DEV = 256
SLOTS = 6
IMAGES = 256
PAIRS = 32768
OTHERS = 32512
TOKENS = 65536
GROUP = 512
N_EXPERT = 64
N_LOOP = 4


def draw_expert_quota(key, part):
    key = jax.random.fold_in(key, 7)
    key_values, key_pick = jax.random.split(key)
    values = jax.random.randint(key_values, (EXPERTS,), max(1, SLOTS // 2), SLOTS + 1)
    chosen = jax.random.randint(key_pick, (), 0, EXPERTS)
    return jnp.where(jnp.arange(EXPERTS) == chosen, SLOTS, values).astype(jnp.int32)


def touch_ends(values, rng, smallest, high):
    longest = values.shape.index(max(values.shape))
    spots = []
    for shift in (0, 1):
        where = [jax.random.randint(jax.random.fold_in(rng, axis), (), 0, length) for axis, length in enumerate(values.shape)]
        where[longest] = (where[longest] + shift) % values.shape[longest]
        spots.append(tuple(where))
    return values.at[spots[0]].set(smallest).at[spots[1]].set(high)


def level_of(rng, dims, cuts, smallest, high):
    level = 1.0
    for position, blocks in cuts:
        heights = jax.random.uniform(jax.random.fold_in(jax.random.fold_in(rng, 6), position), (blocks,), jnp.float32, smallest / len(cuts), high / len(cuts))
        level = level * jnp.repeat(jnp.exp(heights), dims[position] // blocks).reshape((-1,) + (1,) * (len(dims) - 1 - position))
    return level


def deal_out(stream_key, own, number, rows, amount, top, limit, lean):
    ranking = jax.random.permutation(stream_key, amount)
    packed, common = load_shares(amount, rows * top, limit, lean, True), load_shares(amount, rows * top, limit, lean, False)
    places = jnp.arange(amount)

    def named(lengths, rotation):
        used = int((lengths > 0).sum())
        fixed = max(1, used // 4)
        passed = fixed + (places - fixed + rotation * (used - fixed)) % max(1, amount - fixed)
        return jnp.zeros((amount,), jnp.int32).at[ranking[jnp.where(places < fixed, places, passed)]].set(jnp.asarray(lengths, jnp.int32))

    lengths = jnp.where(number % 4 == 0, named(packed, number // 4), named(common, number - number // 4 - 1))
    mixed = jax.random.permutation(jax.random.fold_in(own, 3), amount)
    source_of, taker = mixed[0:amount // 2 * 2:2], mixed[1:amount // 2 * 2:2]
    room = jnp.minimum(lengths[source_of] - 1, limit - lengths[taker]) // 2
    room = jnp.where((source_of == ranking[0]) | (taker == ranking[0]) | (lengths[taker] == 0), 0, jnp.maximum(room, 0))
    passed = jax.random.randint(jax.random.fold_in(own, 4), (amount // 2,), 0, 1 << 20) % (room + 1)
    lengths = lengths.at[source_of].add(-passed).at[taker].add(passed)
    items = jnp.searchsorted(jnp.cumsum(lengths), jnp.arange(rows * top), side="right").astype(jnp.int32)
    grid = items.reshape(top, rows).T
    grid = grid[jax.random.permutation(jax.random.fold_in(own, 1), rows)]
    rotation = jax.random.randint(jax.random.fold_in(own, 2), (rows, 1), 0, top)
    return jnp.take_along_axis(grid, (jnp.arange(top)[None, :] + rotation) % top, axis=1)


def load_shares(amount, total, bound, skew, full):
    loads = [(1 << 20) // math.isqrt(standing ** skew) + 1 for standing in range(1, amount + 1)]
    largest = bound if full else min(bound, max(-(-total // amount), total * loads[0] // sum(loads)))
    least = 1 if total - largest >= amount - 1 else 0
    holding, rest = [largest] + [least] * (amount - 1), total - largest - least * (amount - 1)
    while rest > 0:
        free = [i for i in range(1, amount) if holding[i] < largest] or [i for i in range(1, amount) if holding[i] < bound]
        pool, left = sum([loads[i] for i in free]), rest
        for i in free:
            more = min(bound - holding[i], max(1, left * loads[i] // pool), rest)
            holding[i] = holding[i] + more
            rest = rest - more
    return np.array(holding)


def bell_draw(own_key, shape, scale, bound, pieces=(), kind=jnp.bfloat16):
    entries = jax.random.normal(own_key, shape, jnp.float32) * scale
    if len(pieces) > 0:
        entries = level_of(own_key, shape, pieces, -0.22, 0.18) * entries
    return jnp.clip(entries, min=-bound, max=bound).astype(kind)


def setup_inputs(seed: int = 0) -> dict:
    key_list = jax.random.split(jax.random.key(seed), 11)
    tokens = bell_draw(key_list[0], (TOKENS, D), 1.0, 6.0, ((0, 256),))
    routes_keys = jax.random.split(jax.random.fold_in(key_list[1], 1), TOKENS // TOK_DEV)
    routes_turns = jax.random.permutation(jax.random.fold_in(key_list[1], 3), TOKENS // TOK_DEV)
    routes = jax.vmap(lambda own, number: deal_out(jax.random.fold_in(key_list[1], 2), own, number, TOK_DEV, EXPERTS, TOP, SLOTS, 2))(routes_keys, routes_turns).reshape((TOKENS, TOP))
    gate_prob = jnp.clip(0.2 + 0.8 * jax.random.uniform(key_list[2], (TOKENS,), jnp.float32) ** level_of(key_list[2], (TOKENS,), ((0, 256),), -0.2, 0.2), 0.2, 1.0)
    expert_quota = draw_expert_quota(jax.random.fold_in(key_list[10], 71), 0)
    w_in = bell_draw(key_list[4], (EXPERTS, D, FF), D ** -0.5, 0.15625, ((0, 64), (2, 4)))
    w_out = bell_draw(key_list[5], (EXPERTS, D, FF), FF ** -0.5, 0.078125, ((0, 64), (2, 4)))
    other_pooled = bell_draw(key_list[6], (OTHERS, D), 1.0, 6.0, ((0, 256),))
    head = bell_draw(key_list[7], (D, EMBED), D ** -0.5, 0.15625)
    text_embed = bell_draw(key_list[8], (PAIRS, EMBED), 1.0, 6.0, ((0, 256),))
    labels = touch_ends(jax.random.randint(key_list[9], (PAIRS,), 0, 4), jax.random.fold_in(key_list[9], 1), 0, 3).astype(jnp.int32)
    return {"tokens": tokens, "routes": routes, "gate_prob": gate_prob, "expert_quota": expert_quota, "w_in": w_in, "w_out": w_out, "other_pooled": other_pooled, "head": head, "text_embed": text_embed, "labels": labels}


scale_logit = 4.0
shift_logit = -1.0

def reference(tokens, routes, gate_prob, expert_quota, w_in, w_out, other_pooled, head, text_embed, labels):
    sources = N_EXPERT * N_LOOP
    block_hidden = FF // N_LOOP
    expert_ids = routes[:, 0].reshape(sources, TOK_DEV)
    onehot = (expert_ids[:, :, None] == jnp.arange(EXPERTS, dtype=jnp.int32)[None, None, :]).astype(jnp.int32)
    slot = lax.optimization_barrier(jnp.sum((jnp.cumsum(onehot, axis=1) - 1) * onehot, axis=2))
    quota_tok = lax.optimization_barrier(jnp.sum(onehot * expert_quota[None, None, :], axis=2))
    kept = slot < quota_tok
    slot_safe = jnp.where(kept, slot, SLOTS).astype(jnp.int32)
    token_ids = jnp.arange(TOKENS, dtype=jnp.int32).reshape(sources, TOK_DEV)
    source_ids = jnp.broadcast_to(jnp.arange(sources, dtype=jnp.int32)[:, None], (sources, TOK_DEV))
    table = jnp.full((EXPERTS, sources, SLOTS), TOKENS, jnp.int32)
    table = table.at[expert_ids, source_ids, slot_safe].set(token_ids, mode='drop')
    padded = jnp.concatenate([tokens, jnp.zeros((1, D), jnp.bfloat16)], axis=0)

    def one_expert(carry, items):
        index_rows, first, second = items
        flat_index = index_rows.reshape(-1)
        rows = padded[flat_index].astype(jnp.float32)
        first_blocks = first.reshape(D, N_LOOP, block_hidden).astype(jnp.float32)
        second_blocks = second.reshape(D, N_LOOP, block_hidden).astype(jnp.float32)
        hidden = jax.nn.gelu(jnp.einsum('rd,dgf->grf', rows, first_blocks)).astype(jnp.bfloat16)
        hidden = lax.optimization_barrier(hidden).astype(jnp.float32)
        parts = jnp.einsum('grf,dgf->grd', hidden, second_blocks).astype(jnp.bfloat16)
        parts = lax.optimization_barrier(parts).astype(jnp.float32)
        result = lax.optimization_barrier(jnp.sum(parts, axis=0)).astype(jnp.bfloat16)
        carry = carry.at[flat_index].add(result.astype(jnp.float32))
        return (carry, None)
    contrib, _ = lax.scan(one_expert, jnp.zeros((TOKENS + 1, D), jnp.float32), (table, w_in, w_out))
    layer = tokens.astype(jnp.float32) + gate_prob[:, None] * contrib[:TOKENS]
    layer_out = layer.astype(jnp.bfloat16)
    own = lax.optimization_barrier(jnp.mean(layer.reshape(IMAGES, PATCHES, D), axis=1)).astype(jnp.bfloat16)
    pooled = jnp.concatenate([own.reshape(IMAGES, 1, D), other_pooled.reshape(IMAGES, PAIRS_DEV - 1, D)], axis=1).reshape(PAIRS, D)
    projected = jnp.dot(pooled, head, preferred_element_type=jnp.float32)
    image = (projected / jnp.sqrt(lax.optimization_barrier(jnp.sum(projected * projected, axis=1, keepdims=True)) + 1e-06)).astype(jnp.bfloat16)
    text_raw = text_embed.astype(jnp.float32)
    text = (text_raw / jnp.sqrt(lax.optimization_barrier(jnp.sum(text_raw * text_raw, axis=1, keepdims=True)) + 1e-06)).astype(jnp.bfloat16)
    batches = PAIRS // GROUP
    image_b = image.reshape(batches, GROUP, EMBED).astype(jnp.float32)
    text_b = text.reshape(batches, GROUP, EMBED).astype(jnp.float32)
    label_b = labels.reshape(batches, GROUP)
    logit = scale_logit * jnp.einsum('gik,gjk->gij', image_b, text_b) + shift_logit
    sign = jnp.where(label_b[:, :, None] == label_b[:, None, :], 1.0, -1.0).astype(jnp.float32)
    loss_rows = lax.optimization_barrier(jnp.sum(jax.nn.softplus(-sign * logit), axis=2)).reshape(PAIRS)
    coef = (-scale_logit * sign * jax.nn.sigmoid(-sign * logit)).astype(jnp.bfloat16).astype(jnp.float32)
    image_grad = jnp.einsum('gij,gjk->gik', coef, text_b).reshape(PAIRS, EMBED)
    text_grad = jnp.einsum('gij,gik->gjk', coef, image_b).reshape(PAIRS, EMBED)
    return (layer_out, loss_rows, image_grad, text_grad)
```

```python
import jax
import jax.numpy as jnp
from jax import lax
from jax.sharding import PartitionSpec as P

PATCHES = 256
PAIRS = 128
LOOP = 4

scale_logit = 4.0
shift_logit = -1.0


def normalize_rows(values):
    return values / jnp.sqrt(jnp.sum(values * values, axis=1, keepdims=True) + 1e-06)


def coefficients(logit, sign):
    return (-scale_logit * sign * jax.nn.sigmoid(-sign * logit)).astype(jnp.bfloat16)


def signs(rows, columns):
    return jnp.where(rows[:, None] == columns[None, :], 1.0, -1.0).astype(jnp.float32)


def logits(rows, columns):
    return (
        scale_logit
        * lax.dot_general(
            rows, columns, (((1,), (1,)), ((), ())), preferred_element_type=jnp.float32
        )
        + shift_logit
    )


def shards(
    tokens, routes, gate_prob, expert_quota, w_in, w_out, other_pooled, head, text_embed, labels
):
    experts = lax.axis_size("expert")
    tok_rows = tokens.shape[0]
    width = tokens.shape[1]
    embed = head.shape[1]
    slots = max(2, 3 * tok_rows // (2 * experts))

    pooled = jnp.concatenate([jnp.zeros((1, width), jnp.bfloat16), other_pooled], axis=0)
    image = normalize_rows(jnp.dot(pooled, head, preferred_element_type=jnp.float32)).astype(
        jnp.bfloat16
    )
    text = normalize_rows(text_embed.astype(jnp.float32)).astype(jnp.bfloat16)
    label_values = labels.astype(jnp.bfloat16)
    label_rows = jnp.pad(label_values[None, :], ((0, 7), (0, embed - PAIRS)))
    packed = jnp.concatenate([text, image, label_rows], axis=0)
    gathered = lax.all_gather(packed, "loop", axis=0)

    expert_ids = routes[:, 0]
    onehot = (expert_ids[:, None] == jnp.arange(experts, dtype=jnp.int32)[None, :]).astype(
        jnp.int32
    )
    slot = jnp.sum((jnp.cumsum(onehot, axis=0) - 1) * onehot, axis=1)
    quota_tok = jnp.sum(onehot * expert_quota[None, :], axis=1)
    position = jnp.where(slot < quota_tok, expert_ids * slots + slot, -1)
    placing = (position[:, None] == jnp.arange(experts * slots, dtype=jnp.int32)[None, :]).astype(
        jnp.bfloat16
    )
    outgoing = lax.dot_general(
        placing, tokens, (((0,), (0,)), ((), ())), preferred_element_type=jnp.float32
    )
    outgoing = outgoing.astype(jnp.bfloat16).reshape(experts, slots, width)
    received = lax.all_to_all(outgoing, "expert", split_axis=0, concat_axis=0, tiled=True).reshape(
        experts * slots, width
    )
    received, gathered = lax.optimization_barrier((received, gathered))
    first_local = w_in[0]
    second_local = w_out[0]
    hidden = jax.nn.gelu(
        jnp.dot(
            lax.all_gather(received, "loop", axis=0, tiled=True),
            first_local,
            preferred_element_type=jnp.float32,
        )
    ).astype(jnp.bfloat16)
    term = lax.dot_general(
        hidden, second_local, (((1,), (1,)), ((), ())), preferred_element_type=jnp.float32
    )
    term = lax.optimization_barrier(term.astype(jnp.bfloat16))
    result = lax.psum_scatter(
        term.astype(jnp.float32).astype(jnp.bfloat16), "loop", scatter_dimension=0, tiled=True
    )

    their_text = gathered[:, :PAIRS].reshape(LOOP * PAIRS, embed)
    their_image = gathered[:, PAIRS : 2 * PAIRS].reshape(LOOP * PAIRS, embed)
    their_label = gathered[:, 2 * PAIRS, :PAIRS].reshape(LOOP * PAIRS)
    logit_mine = logits(image, their_text)
    sign_mine = signs(label_values, their_label)
    loss_acc = jnp.sum(jax.nn.softplus(-sign_mine * logit_mine), axis=1)
    image_acc = jnp.dot(
        coefficients(logit_mine, sign_mine), their_text, preferred_element_type=jnp.float32
    )
    coef_their = coefficients(logits(their_image, text), signs(their_label, label_values))
    text_acc = lax.dot_general(
        coef_their, their_image, (((0,), (0,)), ((), ())), preferred_element_type=jnp.float32
    )

    going_back = result.reshape(experts, slots, width)
    returned = lax.all_to_all(
        going_back, "expert", split_axis=0, concat_axis=0, tiled=True
    ).reshape(experts * slots, width)
    contrib = jnp.dot(placing, returned, preferred_element_type=jnp.float32)
    layer = tokens.astype(jnp.float32) + gate_prob[:, None] * contrib
    layer_out = layer.astype(jnp.bfloat16)
    own = jnp.mean(layer.reshape(-1, PATCHES, width), axis=1).astype(jnp.bfloat16)

    own_image = normalize_rows(jnp.dot(own, head, preferred_element_type=jnp.float32)).astype(
        jnp.bfloat16
    )
    me = lax.axis_index("loop")
    own_images = [own_image] + [
        lax.ppermute(own_image, "loop", [(i, (i + step) % LOOP) for i in range(LOOP)])
        for step in range(1, LOOP)
    ]
    own_images = jnp.concatenate(own_images, axis=0)
    first_labels = their_label.reshape(LOOP, PAIRS)[:, 0]
    own_labels = jnp.take(first_labels, (me - jnp.arange(LOOP)) % LOOP)
    own_logit = logits(own_image, their_text)
    own_sign = signs(label_values[:1], their_label)
    own_loss = jnp.sum(jax.nn.softplus(-own_sign * own_logit), axis=1)
    own_grad = jnp.dot(
        coefficients(own_logit, own_sign), their_text, preferred_element_type=jnp.float32
    )
    coef_own = coefficients(logits(own_images, text), signs(own_labels, label_values))
    text_acc = text_acc + lax.dot_general(
        coef_own, own_images, (((0,), (0,)), ((), ())), preferred_element_type=jnp.float32
    )
    loss_acc = lax.dynamic_update_slice(loss_acc, own_loss, (0,))
    image_acc = lax.dynamic_update_slice(image_acc, own_grad, (0, 0))
    return (layer_out, loss_acc, image_acc, text_acc)


def solution(mesh):
    rows = P(("expert", "loop"), None)
    flat = P(("expert", "loop"))
    weights = P("expert", None, "loop")
    in_specs = (rows, rows, flat, P(), weights, weights, rows, P(), rows, flat)
    out_specs = (rows, flat, rows, rows)
    return jax.shard_map(shards, mesh=mesh, in_specs=in_specs, out_specs=out_specs, check_vma=False)
```

```python
import functools

import jax
import jax.numpy as jnp
import numpy as np
from jax import lax
from jax.experimental import pallas as pl
from jax.experimental.pallas import tpu as pltpu
from jax.sharding import Mesh
from jax.sharding import PartitionSpec as P

PATCHES = 256
PAIRS = 128
LOOP = 4
RING = 8
PLANE = 32
SLOTS = 6
EXPERTS = 64
GROUPS = 4
PIECE = 48
BLOCK = PLANE * SLOTS
TOK = 256
ROWS = TOK + 16
SHARD = 2 * PAIRS + 16

AXES = ("zh", "y", "x", "c", "zl")
EXPERT = ("zh", "y", "x", "c")
FLAT = ("y", "x", "c")
Z = ("zh", "zl")

scale_logit = 4.0
shift_logit = -1.0

F32 = jnp.float32
BF16 = jnp.bfloat16


def call(kernel, out_shape, scratch=(), aliases=None, flops=0, vmem=24):
    return pl.pallas_call(
        kernel,
        out_shape=out_shape,
        scratch_shapes=list(scratch),
        input_output_aliases=aliases or {},
        cost_estimate=pl.CostEstimate(flops=flops, bytes_accessed=4 << 20, transcendentals=0),
        compiler_params=pltpu.CompilerParams(vmem_limit_bytes=vmem << 20),
    )


def struct(shape, dtype):
    return jax.ShapeDtypeStruct(shape, dtype)


def iota(shape, dim):
    return lax.broadcasted_iota(jnp.int32, shape, dim)


def dot(a, b):
    return jnp.dot(a, b, preferred_element_type=F32)


def dot_t(a, b):
    return lax.dot_general(a, b, (((1,), (1,)), ((), ())), preferred_element_type=F32)


def as_row(column):
    n = column.shape[0]
    return jnp.sum(jnp.where(iota((n, n), 0) == iota((n, n), 1), column, 0.0), 0, keepdims=True)


def as_column(row):
    n = row.shape[1]
    return jnp.sum(jnp.where(iota((n, n), 0) == iota((n, n), 1), row, 0.0), 1, keepdims=True)


def normalize_rows(values):
    return values / jnp.sqrt(jnp.sum(values * values, axis=1, keepdims=True) + 1e-06)


def softplus(x):
    return jnp.maximum(x, 0.0) + jnp.log1p(jnp.exp(-jnp.abs(x)))


def coefficients(logit, sign):
    return (-scale_logit * sign * lax.logistic(-sign * logit)).astype(BF16)


def sign_of(a, b):
    return jnp.where(a == b, 1.0, -1.0)


def swap_matrix():
    order = np.arange(8 * PIECE).reshape(8, 8, SLOTS).transpose(1, 0, 2).reshape(-1)
    return np.eye(8 * PIECE, dtype=np.float32)[order].astype(jnp.bfloat16)


def half_matrix():
    order = np.arange(2 * BLOCK).reshape(PLANE, 2, SLOTS).transpose(1, 0, 2).reshape(-1)
    return np.eye(2 * BLOCK, dtype=np.float32)[order].astype(jnp.bfloat16)


def route_kernel(tokens, routes, quota, packed, outgoing, position):
    half = packed.shape[1]
    ids = routes[...]
    hit = ids == iota((TOK, EXPERTS), 1)
    onehot = jnp.where(hit, 1.0, 0.0)
    before = dot(
        jnp.where(iota((TOK, TOK), 1) < iota((TOK, TOK), 0), 1.0, 0.0).astype(BF16),
        onehot.astype(BF16),
    )
    slot = jnp.sum(onehot * before, axis=1, keepdims=True)
    limit = jnp.sum(onehot * quota[...].astype(F32), axis=1, keepdims=True)
    kept = slot < limit
    far = jnp.where(ids >= PLANE, 1, 0)
    place = (ids - far * PLANE) * (2 * SLOTS) + far * SLOTS
    column = jnp.where(kept, place.astype(F32) + slot, -1.0)
    position[...] = column
    id_row = as_row(ids.astype(F32))
    slot_row = as_row(jnp.where(kept, slot, 64.0))
    line = iota((16, TOK), 0)
    packed[0:TOK, :] = tokens[:, :half]
    packed[TOK:ROWS, :] = jnp.zeros((16, half), BF16)
    packed[TOK:ROWS, 0:TOK] = jnp.where(
        line == 0, id_row, jnp.where(line == 1, slot_row, 0.0)
    ).astype(BF16)
    place = as_row(column).astype(jnp.int32)
    onto = jnp.where(iota((EXPERTS * SLOTS, TOK), 0) == place, 1.0, 0.0).astype(BF16)
    outgoing[...] = dot(onto, tokens[:, half:]).astype(BF16)


def choose_kernel(gathered, side, swap, chosen, target, held):
    first = side[0, 0].astype(F32) * PLANE
    for z in range(RING):
        info = gathered[z * ROWS + TOK : (z + 1) * ROWS, 0:TOK].astype(F32)
        ids = info[0:1] - first
        slot = info[1:2]
        mine = (ids >= 0.0) & (ids < float(PLANE)) & (slot < float(SLOTS))
        row = jnp.where(mine, ids * SLOTS + slot, -1.0)
        target[z : z + 1, :] = row
        onto = jnp.where(iota((BLOCK, TOK), 0) == row.astype(jnp.int32), 1.0, 0.0).astype(BF16)
        held[z * BLOCK : (z + 1) * BLOCK, :] = dot(
            onto, gathered[z * ROWS : z * ROWS + TOK, :]
        ).astype(BF16)
    for g in range(GROUPS):
        rows = jnp.concatenate(
            [held[z * BLOCK + g * PIECE : z * BLOCK + (g + 1) * PIECE, :] for z in range(RING)], 0
        )
        chosen[g * 8 * PIECE : (g + 1) * 8 * PIECE, :] = dot(swap[...], rows).astype(BF16)


def spread_kernel(rows, swap, out):
    for g in range(GROUPS):
        moved = dot(swap[...], rows[g * 8 * PIECE : (g + 1) * 8 * PIECE, :]).astype(BF16)
        for z in range(RING):
            at = z * BLOCK + g * PIECE
            out[at : at + PIECE, :] = moved[z * PIECE : (z + 1) * PIECE, :]


def unspread_kernel(rows, swap, out):
    for g in range(GROUPS):
        starts = [z * BLOCK + g * PIECE for z in range(RING)]
        piece = jnp.concatenate([rows[at : at + PIECE, :] for at in starts], 0)
        out[g * 8 * PIECE : (g + 1) * 8 * PIECE, :] = dot(swap[...], piece).astype(BF16)


def turn_kernel(rows, matrix, out):
    out[...] = dot(matrix[...], rows[...]).astype(BF16)


def expert_kernel(side, rows, partial, first, second, hidden, term):
    x = jnp.concatenate([rows[0, 0], rows[1, 0]], 0)
    value = jax.nn.gelu(partial[...] + dot(x, first[...])).astype(BF16)
    hidden[...] = value
    result = dot_t(value, second[...]).astype(BF16)
    nothing = jnp.zeros((BLOCK, result.shape[1]), BF16)
    for k in range(2):
        mine = result[k * BLOCK : (k + 1) * BLOCK]
        for far in range(2):
            term[k, far] = jnp.where(side[0] == far, mine, nothing)


def expert_right(side, rows, partial, first, second):
    half, inner = first.shape
    spec = pl.BlockSpec
    return pl.pallas_call(
        expert_kernel,
        out_shape=(
            struct((RING * BLOCK, inner), BF16),
            struct((RING, 2, BLOCK, half), BF16),
        ),
        grid_spec=pltpu.PrefetchScalarGridSpec(
            num_scalar_prefetch=1,
            grid=(RING // 2,),
            in_specs=[
                spec((2, 1, BLOCK, half), lambda i, side: (i, side[0], 0, 0)),
                spec((2 * BLOCK, inner), lambda i, side: (i, 0)),
                spec((half, inner), lambda i, side: (0, 0)),
                spec((half, inner), lambda i, side: (0, 0)),
            ],
            out_specs=[
                spec((2 * BLOCK, inner), lambda i, side: (i, 0)),
                spec((2, 2, BLOCK, half), lambda i, side: (i, 0, 0, 0)),
            ],
        ),
        cost_estimate=pl.CostEstimate(
            flops=4 * RING * BLOCK * half * inner, bytes_accessed=20 << 20, transcendentals=0
        ),
        compiler_params=pltpu.CompilerParams(vmem_limit_bytes=32 << 20),
    )(side, rows, partial, first, second)


def scatter_kernel(rows, swap, target, out, held):
    for g in range(GROUPS):
        moved = dot(swap[...], rows[g * 8 * PIECE : (g + 1) * 8 * PIECE, :]).astype(BF16)
        for z in range(RING):
            at = z * BLOCK + g * PIECE
            held[at : at + PIECE, :] = moved[z * PIECE : (z + 1) * PIECE, :]
    for z in range(RING):
        column = as_column(target[z : z + 1, :]).astype(jnp.int32)
        onto = jnp.where(iota((TOK, BLOCK), 1) == column, 1.0, 0.0).astype(BF16)
        out[z * TOK : (z + 1) * TOK, :] = dot(
            onto, held[z * BLOCK : (z + 1) * BLOCK, :]
        ).astype(BF16)


def layer_kernel(tokens, position, gate, returned, given, head, layer_out, own_image):
    half = given.shape[1]
    onto = jnp.where(
        iota((TOK, EXPERTS * SLOTS), 1) == position[...].astype(jnp.int32), 1.0, 0.0
    ).astype(BF16)
    left = tokens[:, :half].astype(F32) + gate[...] * given[...].astype(F32)
    right = tokens[:, half:].astype(F32) + gate[...] * dot(onto, returned[...])
    layer_out[:, :half] = left.astype(BF16)
    layer_out[:, half:] = right.astype(BF16)
    own_left = (jnp.sum(left, axis=0, keepdims=True) / PATCHES).astype(BF16)
    own_right = (jnp.sum(right, axis=0, keepdims=True) / PATCHES).astype(BF16)
    own_left = jnp.broadcast_to(own_left.astype(F32), (16, half)).astype(BF16)
    own_right = jnp.broadcast_to(own_right.astype(F32), (16, half)).astype(BF16)
    image = dot(own_left, head[:half, :]) + dot(own_right, head[half:, :])
    own_image[...] = normalize_rows(image)[0:1].astype(BF16)


def pack_kernel(pooled, head, text_embed, labels, packed):
    packed[0:PAIRS, :] = normalize_rows(text_embed[...].astype(F32)).astype(BF16)
    image = normalize_rows(dot(pooled[...], head[...]))
    packed[PAIRS : 2 * PAIRS, :] = image.astype(BF16)
    packed[2 * PAIRS : SHARD, :] = jnp.zeros((16, packed.shape[1]), BF16)
    packed[2 * PAIRS : SHARD, 0:PAIRS] = jnp.where(
        iota((16, PAIRS), 0) == 0, labels[...].astype(F32), 0.0
    ).astype(BF16)


def label_row(shard):
    return shard[2 * PAIRS : SHARD, 0:PAIRS].astype(F32)[0:1]


def score_kernel(own, s1, s2, s3, loss, image_acc, text_acc):
    text = own[0:PAIRS, :]
    image = own[PAIRS : 2 * PAIRS, :]
    mine = as_column(label_row(own))
    losses = jnp.zeros((PAIRS, 1), F32)
    for k, shard in enumerate((own, s1, s2, s3)):
        their_text = shard[0:PAIRS, :]
        their_image = shard[PAIRS : 2 * PAIRS, :]
        sign = sign_of(mine, label_row(shard))
        logit = scale_logit * dot_t(image, their_text) + shift_logit
        losses = losses + jnp.sum(softplus(-sign * logit), axis=1, keepdims=True)
        grad = dot(coefficients(logit, sign), their_text)
        logit = scale_logit * dot_t(text, their_image) + shift_logit
        text_grad = dot(coefficients(logit, sign), their_image)
        image_acc[...] = grad if k == 0 else image_acc[...] + grad
        text_acc[...] = text_grad if k == 0 else text_acc[...] + text_grad
    loss[...] = as_row(losses)


def own_row_kernel(own_image, own, s1, s2, s3, loss, image_acc, loss_out, image_out):
    row = jnp.broadcast_to(own_image[...].astype(F32), (16, own_image.shape[1])).astype(BF16)
    label = label_row(own)[0:1, 0:1]
    total = jnp.zeros((16, 1), F32)
    grad = jnp.zeros((16, own_image.shape[1]), F32)
    for shard in (own, s1, s2, s3):
        their_text = shard[0:PAIRS, :]
        sign = sign_of(label, label_row(shard))
        logit = scale_logit * dot_t(row, their_text) + shift_logit
        total = total + jnp.sum(softplus(-sign * logit), axis=1, keepdims=True)
        grad = grad + dot(coefficients(logit, sign), their_text)
    loss_out[...] = jnp.where(iota((1, PAIRS), 1) == 0, total[0:1], loss[...])
    image_out[...] = image_acc[...]
    image_out[0:1, :] = grad[0:1]


def own_text_kernel(i0, i1, i2, i3, own, s1, s2, s3, text_acc, out):
    line = iota((16, i0.shape[1]), 0)
    images = jnp.zeros((16, i0.shape[1]), F32)
    for k, row in enumerate((i0, i1, i2, i3)):
        images = jnp.where(line == k, row[...].astype(F32), images)
    images = images.astype(BF16)
    place = iota((1, 16), 1)
    labels = jnp.full((1, 16), -1.0, F32)
    for k, shard in enumerate((own, s1, s2, s3)):
        labels = jnp.where(place == k, label_row(shard)[0:1, 0:1], labels)
    sign = sign_of(as_column(label_row(own)), labels)
    logit = scale_logit * dot_t(own[0:PAIRS, :], images) + shift_logit
    out[...] = text_acc[...] + dot(coefficients(logit, sign), images)


def shards(
    tokens, routes, gate_prob, expert_quota, w_in, w_out, other_pooled, head, text_embed, labels
):
    width = tokens.shape[1]
    half = width // 2
    embed = head.shape[1]
    swap = jnp.asarray(swap_matrix())
    apart = jnp.asarray(half_matrix())
    together = jnp.asarray(half_matrix().T)
    side = lax.axis_index("zh").astype(jnp.int32).reshape(1, 1)

    packed, outgoing, position = call(
        route_kernel,
        (
            struct((ROWS, half), BF16),
            struct((EXPERTS * SLOTS, half), BF16),
            struct((TOK, 1), F32),
        ),
        flops=1 << 28,
    )(tokens, routes, expert_quota.reshape(1, EXPERTS))

    pooled = jnp.concatenate([jnp.zeros((1, width), BF16), other_pooled], axis=0)
    own_pairs = call(pack_kernel, struct((SHARD, embed), BF16), flops=1 << 28)(
        pooled, head, text_embed, labels.reshape(1, PAIRS)
    )
    shift = lambda value, step: lax.ppermute(
        value, "zl", [(i, (i + step) % LOOP) for i in range(LOOP)]
    )

    around = lax.all_gather(packed, Z, axis=0, tiled=True)
    received = lax.all_to_all(
        outgoing.reshape(PLANE, 2 * SLOTS, half), FLAT, split_axis=0, concat_axis=0, tiled=True
    ).reshape(2 * BLOCK, half)
    received = call(turn_kernel, struct((2 * BLOCK, half), BF16), flops=1 << 28)(received, apart)
    received, around, own_pairs = lax.optimization_barrier((received, around, own_pairs))
    right = lax.all_gather(received, Z, axis=0, tiled=True)

    chosen, target = call(
        choose_kernel,
        (struct((RING * BLOCK, half), BF16), struct((RING, TOK), F32)),
        scratch=[pltpu.VMEM((RING * BLOCK, half), BF16)],
        flops=1 << 30,
    )(around, side, swap)
    arrived = lax.all_to_all(
        chosen.reshape(PLANE, PIECE, half), FLAT, split_axis=0, concat_axis=0, tiled=True
    ).reshape(RING * BLOCK, half)
    left = call(spread_kernel, struct((RING * BLOCK, half), BF16), flops=1 << 30)(arrived, swap)

    first = w_in[0]
    second = w_out[0]
    partial = dot(left, first[:half])
    partial, own_pairs = lax.optimization_barrier((partial, own_pairs))
    pairs = [own_pairs] + [shift(own_pairs, step) for step in range(1, LOOP)]
    hidden, term_right = expert_right(
        side.reshape(1), right.reshape(RING, 2, BLOCK, half), partial, first[half:], second[half:]
    )
    hidden, term_right, pairs[1] = lax.optimization_barrier((hidden, term_right, pairs[1]))
    result = lax.psum_scatter(
        term_right.reshape(2 * RING * BLOCK, half), Z, scatter_dimension=0, tiled=True
    )
    term_left = lax.optimization_barrier(dot_t(hidden, second[:half]).astype(BF16))
    leaving = call(unspread_kernel, struct((RING * BLOCK, half), BF16), flops=1 << 30)(
        term_left, swap
    )
    back = lax.all_to_all(
        leaving.reshape(PLANE, PIECE, half), FLAT, split_axis=0, concat_axis=0, tiled=True
    ).reshape(RING * BLOCK, half)
    back, result, *pairs = lax.optimization_barrier((back, result, *pairs))
    by_token = call(
        scatter_kernel,
        struct((RING * TOK, half), BF16),
        scratch=[pltpu.VMEM((RING * BLOCK, half), BF16)],
        flops=1 << 30,
    )(back, swap, target)
    given = lax.psum_scatter(by_token, Z, scatter_dimension=0, tiled=True)
    result = call(turn_kernel, struct((2 * BLOCK, half), BF16), flops=1 << 28)(result, together)
    returned = lax.all_to_all(
        result.reshape(PLANE, 2 * SLOTS, half), FLAT, split_axis=0, concat_axis=0, tiled=True
    ).reshape(2 * BLOCK, half)

    square = struct((PAIRS, embed), F32)
    line = struct((1, PAIRS), F32)
    loss, image_acc, text_acc = call(score_kernel, (line, square, square), flops=1 << 30)(*pairs)
    loss, image_acc, text_acc, returned = lax.optimization_barrier(
        (loss, image_acc, text_acc, returned)
    )

    layer_out, own_image = call(
        layer_kernel, (struct((TOK, width), BF16), struct((1, embed), BF16)), flops=1 << 28
    )(tokens, position, gate_prob.reshape(TOK, 1), returned, given, head)
    own_images = [own_image] + [shift(own_image, step) for step in range(1, LOOP)]
    loss, image_acc = call(own_row_kernel, (line, square), flops=1 << 26)(
        own_image, *pairs, loss, image_acc
    )
    text_acc = call(own_text_kernel, square, flops=1 << 26)(*own_images, *pairs, text_acc)
    return (layer_out, loss.reshape(PAIRS), image_acc, text_acc)


def solution(mesh):
    fine = Mesh(mesh.devices.reshape(2, 4, 4, 2, LOOP), AXES)
    rows = P(AXES, None)
    flat = P(AXES)
    weights = P(EXPERT, None, "zl")
    in_specs = (rows, rows, flat, P(), weights, weights, rows, P(), rows, flat)
    out_specs = (rows, flat, rows, rows)
    return jax.shard_map(shards, mesh=fine, in_specs=in_specs, out_specs=out_specs, check_vma=False)
```

```python
import functools

import jax
import jax.numpy as jnp
import numpy as np
from jax import lax
from jax.experimental import pallas as pl
from jax.experimental.pallas import tpu as pltpu
from jax.sharding import Mesh
from jax.sharding import PartitionSpec as P

PATCHES = 256
PAIRS = 128
LOOP = 4
RING = 8
PLANE = 32
SLOTS = 6
EXPERTS = 64
GROUPS = 4
PIECE = 48
BLOCK = PLANE * SLOTS
TOK = 256
ROWS = TOK + 16
SHARD = 2 * PAIRS + 16

AXES = ("zh", "y", "x", "c", "zl")
EXPERT = ("zh", "y", "x", "c")
FLAT = ("y", "x", "c")
Z = ("zh", "zl")

scale_logit = 4.0
shift_logit = -1.0

F32 = jnp.float32
BF16 = jnp.bfloat16


def call(kernel, out_shape, scratch=(), aliases=None, flops=0, vmem=60):
    return pl.pallas_call(
        kernel,
        out_shape=out_shape,
        scratch_shapes=list(scratch),
        input_output_aliases=aliases or {},
        cost_estimate=pl.CostEstimate(flops=flops, bytes_accessed=4 << 20, transcendentals=0),
        compiler_params=pltpu.CompilerParams(vmem_limit_bytes=vmem << 20),
    )


def struct(shape, dtype):
    return jax.ShapeDtypeStruct(shape, dtype)


def iota(shape, dim):
    return lax.broadcasted_iota(jnp.int32, shape, dim)


def dot(a, b):
    return jnp.dot(a, b, preferred_element_type=F32)


def dot_t(a, b):
    return lax.dot_general(a, b, (((1,), (1,)), ((), ())), preferred_element_type=F32)


def as_row(column):
    n = column.shape[0]
    return jnp.sum(jnp.where(iota((n, n), 0) == iota((n, n), 1), column, 0.0), 0, keepdims=True)


def as_column(row):
    n = row.shape[1]
    return jnp.sum(jnp.where(iota((n, n), 0) == iota((n, n), 1), row, 0.0), 1, keepdims=True)


def normalize_rows(values):
    return values / jnp.sqrt(jnp.sum(values * values, axis=1, keepdims=True) + 1e-06)


def softplus(x):
    return jnp.maximum(x, 0.0) + jnp.log1p(jnp.exp(-jnp.abs(x)))


def coefficients(logit, sign):
    return (-scale_logit * sign * lax.logistic(-sign * logit)).astype(BF16)


def sign_of(a, b):
    return jnp.where(a == b, 1.0, -1.0)


def swap_matrix():
    order = np.arange(8 * PIECE).reshape(8, 8, SLOTS).transpose(1, 0, 2).reshape(-1)
    return np.eye(8 * PIECE, dtype=np.float32)[order].astype(jnp.bfloat16)


def half_matrix():
    order = np.arange(2 * BLOCK).reshape(PLANE, 2, SLOTS).transpose(1, 0, 2).reshape(-1)
    return np.eye(2 * BLOCK, dtype=np.float32)[order].astype(jnp.bfloat16)


def route_kernel(tokens, routes, quota, packed, outgoing, position):
    half = packed.shape[1]
    ids = as_column(routes[...].astype(F32)).astype(jnp.int32)
    hit = ids == iota((TOK, EXPERTS), 1)
    onehot = jnp.where(hit, 1.0, 0.0)
    before = dot(
        jnp.where(iota((TOK, TOK), 1) < iota((TOK, TOK), 0), 1.0, 0.0).astype(BF16),
        onehot.astype(BF16),
    )
    slot = jnp.sum(onehot * before, axis=1, keepdims=True)
    limit = jnp.sum(onehot * quota[...].astype(F32), axis=1, keepdims=True)
    kept = slot < limit
    far = jnp.where(ids >= PLANE, 1, 0)
    place = (ids - far * PLANE) * (2 * SLOTS) + far * SLOTS
    column = jnp.where(kept, place.astype(F32) + slot, -1.0)
    placing = as_row(column)
    position[...] = placing
    id_row = as_row(ids.astype(F32))
    slot_row = as_row(jnp.where(kept, slot, 64.0))
    line = iota((16, TOK), 0)
    packed[0:TOK, :] = tokens[:, :half]
    packed[TOK:ROWS, :] = jnp.zeros((16, half), BF16)
    packed[TOK:ROWS, 0:TOK] = jnp.where(
        line == 0, id_row, jnp.where(line == 1, slot_row, 0.0)
    ).astype(BF16)
    onto = jnp.where(
        iota((EXPERTS * SLOTS, TOK), 0) == placing.astype(jnp.int32), 1.0, 0.0
    ).astype(BF16)
    outgoing[...] = dot(onto, tokens[:, half:]).astype(BF16)


def choose_kernel(gathered, side, swap, chosen, target, held):
    first = side[0, 0].astype(F32) * PLANE
    for z in range(RING):
        info = gathered[z * ROWS + TOK : (z + 1) * ROWS, 0:TOK].astype(F32)
        ids = info[0:1] - first
        slot = info[1:2]
        mine = (ids >= 0.0) & (ids < float(PLANE)) & (slot < float(SLOTS))
        row = jnp.where(mine, ids * SLOTS + slot, -1.0)
        target[z : z + 1, :] = row
        onto = jnp.where(iota((BLOCK, TOK), 0) == row.astype(jnp.int32), 1.0, 0.0).astype(BF16)
        held[z * BLOCK : (z + 1) * BLOCK, :] = dot(
            onto, gathered[z * ROWS : z * ROWS + TOK, :]
        ).astype(BF16)
    for g in range(GROUPS):
        rows = jnp.concatenate(
            [held[z * BLOCK + g * PIECE : z * BLOCK + (g + 1) * PIECE, :] for z in range(RING)], 0
        )
        chosen[g * 8 * PIECE : (g + 1) * 8 * PIECE, :] = dot(swap[...], rows).astype(BF16)


def spread_kernel(rows, swap, out):
    for g in range(GROUPS):
        moved = dot(swap[...], rows[g * 8 * PIECE : (g + 1) * 8 * PIECE, :]).astype(BF16)
        for z in range(RING):
            at = z * BLOCK + g * PIECE
            out[at : at + PIECE, :] = moved[z * PIECE : (z + 1) * PIECE, :]


def unspread_kernel(rows, swap, out):
    for g in range(GROUPS):
        starts = [z * BLOCK + g * PIECE for z in range(RING)]
        piece = jnp.concatenate([rows[at : at + PIECE, :] for at in starts], 0)
        out[g * 8 * PIECE : (g + 1) * 8 * PIECE, :] = dot(swap[...], piece).astype(BF16)


def turn_kernel(rows, matrix, out):
    out[...] = dot(matrix[...], rows[...]).astype(BF16)


def expert_kernel(side, rows, partial, first, second, hidden, term):
    x = jnp.concatenate([rows[0, 0], rows[1, 0]], 0)
    value = jax.nn.gelu(partial[...] + dot(x, first[...])).astype(BF16)
    hidden[...] = value
    result = dot_t(value, second[...]).astype(BF16)
    nothing = jnp.zeros((BLOCK, result.shape[1]), BF16)
    for k in range(2):
        mine = result[k * BLOCK : (k + 1) * BLOCK]
        for far in range(2):
            term[k, far] = jnp.where(side[0] == far, mine, nothing)


def expert_right(side, rows, partial, first, second):
    half, inner = rows.shape[3], first.shape[1]
    spec = pl.BlockSpec
    return pl.pallas_call(
        expert_kernel,
        out_shape=(
            struct((RING * BLOCK, inner), BF16),
            struct((RING, 2, BLOCK, half), BF16),
        ),
        grid_spec=pltpu.PrefetchScalarGridSpec(
            num_scalar_prefetch=1,
            grid=(RING // 2,),
            in_specs=[
                spec((2, 1, BLOCK, half), lambda i, side: (i, side[0], 0, 0)),
                spec((2 * BLOCK, inner), lambda i, side: (i, 0)),
                spec((half, inner), lambda i, side: (1, 0)),
                spec((half, inner), lambda i, side: (1, 0)),
            ],
            out_specs=[
                spec((2 * BLOCK, inner), lambda i, side: (i, 0)),
                spec((2, 2, BLOCK, half), lambda i, side: (i, 0, 0, 0)),
            ],
        ),
        cost_estimate=pl.CostEstimate(
            flops=4 * RING * BLOCK * half * inner, bytes_accessed=20 << 20, transcendentals=0
        ),
        compiler_params=pltpu.CompilerParams(vmem_limit_bytes=60 << 20),
    )(side, rows, partial, first, second)


def scatter_kernel(rows, swap, target, out, held):
    for g in range(GROUPS):
        moved = dot(swap[...], rows[g * 8 * PIECE : (g + 1) * 8 * PIECE, :]).astype(BF16)
        for z in range(RING):
            at = z * BLOCK + g * PIECE
            held[at : at + PIECE, :] = moved[z * PIECE : (z + 1) * PIECE, :]
    for z in range(RING):
        column = as_column(target[z : z + 1, :]).astype(jnp.int32)
        onto = jnp.where(iota((TOK, BLOCK), 1) == column, 1.0, 0.0).astype(BF16)
        out[z * TOK : (z + 1) * TOK, :] = dot(
            onto, held[z * BLOCK : (z + 1) * BLOCK, :]
        ).astype(BF16)


def own_rows(layer):
    own = (jnp.sum(layer, axis=0, keepdims=True) / PATCHES).astype(BF16)
    return jnp.broadcast_to(own.astype(F32), (16, layer.shape[1])).astype(BF16)


def right_kernel(tokens, position, gate, returned, head, layer_out, image):
    column = as_column(position[...]).astype(jnp.int32)
    onto = jnp.where(iota((TOK, EXPERTS * SLOTS), 1) == column, 1.0, 0.0).astype(BF16)
    weight = as_column(gate[...])
    layer = tokens[...].astype(F32) + weight * dot(onto, returned[...])
    layer_out[...] = layer.astype(BF16)
    image[...] = dot(own_rows(layer), head[...])


def left_kernel(tokens, gate, given, head, partial, label, other_half, layer_out, own_image):
    layer = tokens[...].astype(F32) + as_column(gate[...]) * given[...].astype(F32)
    layer_out[...] = layer.astype(BF16)
    image = normalize_rows(partial[...] + dot(own_rows(layer), head[...]))[0:1]
    embed = image.shape[1]
    own_image[:, :embed] = image.astype(BF16)
    own_image[:, embed:] = label[:, 0:128].astype(F32).astype(BF16)


def whole(shape):
    return pl.BlockSpec(shape, lambda i: (0,) * len(shape))


def part(shape, at):
    return pl.BlockSpec(shape, lambda i: at)


def layer_right(tokens, position, gate, returned, head):
    half, embed = returned.shape[1], head.shape[1]
    return pl.pallas_call(
        right_kernel,
        grid=(1,),
        out_shape=(struct(tokens.shape, BF16), struct((16, embed), F32)),
        in_specs=[
            part((TOK, half), (0, 1)),
            whole((1, TOK)),
            whole((1, TOK)),
            whole(returned.shape),
            part((half, embed), (1, 0)),
        ],
        out_specs=(part((TOK, half), (0, 1)), whole((16, embed))),
        cost_estimate=pl.CostEstimate(flops=1 << 28, bytes_accessed=4 << 20, transcendentals=0),
        compiler_params=pltpu.CompilerParams(vmem_limit_bytes=60 << 20),
    )(tokens, position, gate, returned, head)


def layer_left(tokens, gate, given, head, partial, label, right_done):
    half, embed = given.shape[1], head.shape[1]
    return pl.pallas_call(
        left_kernel,
        grid=(1,),
        out_shape=(struct(tokens.shape, BF16), struct((1, embed + 128), BF16)),
        in_specs=[
            part((TOK, half), (0, 0)),
            whole((1, TOK)),
            whole(given.shape),
            part((half, embed), (0, 0)),
            whole((16, embed)),
            whole(label.shape),
            pl.BlockSpec(memory_space=pl.ANY),
        ],
        out_specs=(part((TOK, half), (0, 0)), whole((1, embed + 128))),
        input_output_aliases={6: 0},
        cost_estimate=pl.CostEstimate(flops=1 << 28, bytes_accessed=4 << 20, transcendentals=0),
        compiler_params=pltpu.CompilerParams(vmem_limit_bytes=24 << 20),
    )(tokens, gate, given, head, partial, label, right_done)


def pack_kernel(pooled, head, text_embed, labels, packed):
    packed[0:PAIRS, :] = normalize_rows(text_embed[...].astype(F32)).astype(BF16)
    image = normalize_rows(dot(pooled[...], head[...]))
    packed[PAIRS : 2 * PAIRS, :] = image.astype(BF16)
    packed[2 * PAIRS : SHARD, :] = jnp.zeros((16, packed.shape[1]), BF16)
    packed[2 * PAIRS : SHARD, 0:PAIRS] = jnp.where(
        iota((16, PAIRS), 0) == 0, labels[...].astype(F32), 0.0
    ).astype(BF16)


def label_row(shard):
    return shard[2 * PAIRS : SHARD, 0:PAIRS].astype(F32)[0:1]


def score_kernel(own, s1, s2, s3, loss, image_acc, text_acc):
    text = own[0:PAIRS, :]
    image = own[PAIRS : 2 * PAIRS, :]
    mine = as_column(label_row(own))
    losses = jnp.zeros((PAIRS, 1), F32)
    for k, shard in enumerate((own, s1, s2, s3)):
        their_text = shard[0:PAIRS, :]
        their_image = shard[PAIRS : 2 * PAIRS, :]
        sign = sign_of(mine, label_row(shard))
        logit = scale_logit * dot_t(image, their_text) + shift_logit
        losses = losses + jnp.sum(softplus(-sign * logit), axis=1, keepdims=True)
        grad = dot(coefficients(logit, sign), their_text)
        logit = scale_logit * dot_t(text, their_image) + shift_logit
        text_grad = dot(coefficients(logit, sign), their_image)
        image_acc[...] = grad if k == 0 else image_acc[...] + grad
        text_acc[...] = text_grad if k == 0 else text_acc[...] + text_grad
    loss[...] = as_row(losses)


def own_row_kernel(own_image, own, s1, s2, s3, loss, image_acc, loss_out, image_out):
    embed = own.shape[1]
    row = jnp.broadcast_to(own_image[:, :embed].astype(F32), (16, embed)).astype(BF16)
    label = label_row(own)[0:1, 0:1]
    total = jnp.zeros((16, 1), F32)
    grad = jnp.zeros((16, embed), F32)
    for shard in (own, s1, s2, s3):
        their_text = shard[0:PAIRS, :]
        sign = sign_of(label, label_row(shard))
        logit = scale_logit * dot_t(row, their_text) + shift_logit
        total = total + jnp.sum(softplus(-sign * logit), axis=1, keepdims=True)
        grad = grad + dot(coefficients(logit, sign), their_text)
    loss_out[...] = jnp.where(iota((1, PAIRS), 1) == 0, total[0:1], loss[...])
    image_out[...] = image_acc[...]
    image_out[0:1, :] = grad[0:1]


def own_text_kernel(i0, i1, i2, i3, own, text_acc, out):
    embed = own.shape[1]
    line = iota((16, embed), 0)
    place = iota((1, 16), 1)
    images = jnp.zeros((16, embed), F32)
    labels = jnp.full((1, 16), -1.0, F32)
    for k, row in enumerate((i0, i1, i2, i3)):
        images = jnp.where(line == k, row[:, :embed].astype(F32), images)
        labels = jnp.where(place == k, row[:, embed:].astype(F32)[:, 0:1], labels)
    images = images.astype(BF16)
    sign = sign_of(as_column(label_row(own)), labels)
    logit = scale_logit * dot_t(own[0:PAIRS, :], images) + shift_logit
    out[...] = text_acc[...] + dot(coefficients(logit, sign), images)


def shards(
    tokens, routes, gate_prob, expert_quota, w_in, w_out, other_pooled, head, text_embed, labels
):
    width = tokens.shape[1]
    half = width // 2
    embed = head.shape[1]
    swap = jnp.asarray(swap_matrix())
    apart = jnp.asarray(half_matrix())
    together = jnp.asarray(half_matrix().T)
    side = lax.axis_index("zh").astype(jnp.int32).reshape(1, 1)

    packed, outgoing, position = call(
        route_kernel,
        (
            struct((ROWS, half), BF16),
            struct((EXPERTS * SLOTS, half), BF16),
            struct((1, TOK), F32),
        ),
        flops=1 << 28,
    )(tokens, routes.reshape(1, TOK), expert_quota.reshape(1, EXPERTS))

    pooled = jnp.concatenate([jnp.zeros((1, width), BF16), other_pooled], axis=0)
    own_pairs = call(pack_kernel, struct((SHARD, embed), BF16), flops=1 << 28)(
        pooled, head, text_embed, labels.reshape(1, PAIRS)
    )
    shift = lambda value, step: lax.ppermute(
        value, "zl", [(i, (i + step) % LOOP) for i in range(LOOP)]
    )

    packed, own_pairs = lax.optimization_barrier((packed, own_pairs))

    def onward(right_going, left_going, hops):
        return (
            lax.ppermute(right_going, "zl", [(i, i + 1) for i in range(hops, LOOP - 1)]),
            lax.ppermute(left_going, "zl", [(i, i - 1) for i in range(1, LOOP - hops)]),
        )

    around = lax.all_gather(packed, Z, axis=0, tiled=True)
    received = lax.all_to_all(
        outgoing.reshape(PLANE, 2 * SLOTS, half), FLAT, split_axis=0, concat_axis=0, tiled=True
    ).reshape(2 * BLOCK, half)
    received = call(turn_kernel, struct((2 * BLOCK, half), BF16), flops=1 << 28)(received, apart)
    r1, l1 = onward(own_pairs, own_pairs, 0)
    received, around, r1, l1 = lax.optimization_barrier((received, around, r1, l1))
    right = lax.all_gather(received, Z, axis=0, tiled=True)

    chosen, target = call(
        choose_kernel,
        (struct((RING * BLOCK, half), BF16), struct((RING, TOK), F32)),
        scratch=[pltpu.VMEM((RING * BLOCK, half), BF16)],
        flops=1 << 30,
    )(around, side, swap)
    arrived = lax.all_to_all(
        chosen.reshape(PLANE, PIECE, half), FLAT, split_axis=0, concat_axis=0, tiled=True
    ).reshape(RING * BLOCK, half)
    left = call(spread_kernel, struct((RING * BLOCK, half), BF16), flops=1 << 30)(arrived, swap)

    first = w_in[0]
    second = w_out[0]
    partial = dot(left, first[:half])
    partial, r1, l1 = lax.optimization_barrier((partial, r1, l1))
    r2, l2 = onward(r1, l1, 1)
    hidden, term_right = expert_right(
        side.reshape(1), right.reshape(RING, 2, BLOCK, half), partial, first, second
    )
    hidden, term_right, r2, l2 = lax.optimization_barrier((hidden, term_right, r2, l2))
    r3, l3 = onward(r2, l2, 2)
    result = lax.psum_scatter(
        term_right.reshape(2 * RING * BLOCK, half), Z, scatter_dimension=0, tiled=True
    )
    term_left = lax.optimization_barrier(dot_t(hidden, second[:half]).astype(BF16))
    leaving = call(unspread_kernel, struct((RING * BLOCK, half), BF16), flops=1 << 30)(
        term_left, swap
    )
    leaving, r3, l3 = lax.optimization_barrier((leaving, r3, l3))
    back = lax.all_to_all(
        leaving.reshape(PLANE, PIECE, half), FLAT, split_axis=0, concat_axis=0, tiled=True
    ).reshape(RING * BLOCK, half)
    by_token = call(
        scatter_kernel,
        struct((RING * TOK, half), BF16),
        scratch=[pltpu.VMEM((RING * BLOCK, half), BF16)],
        flops=1 << 30,
    )(back, swap, target)
    by_token, result = lax.optimization_barrier((by_token, result))
    given = lax.psum_scatter(by_token, Z, scatter_dimension=0, tiled=True)
    result = call(turn_kernel, struct((2 * BLOCK, half), BF16), flops=1 << 28)(result, together)
    returned = lax.all_to_all(
        result.reshape(PLANE, 2 * SLOTS, half), FLAT, split_axis=0, concat_axis=0, tiled=True
    ).reshape(2 * BLOCK, half)

    square = struct((PAIRS, embed), F32)
    line = struct((1, PAIRS), F32)
    at = lax.axis_index("zl")
    pairs = [
        own_pairs,
        jnp.where(at == 0, l3, r1),
        jnp.where(at <= 1, l2, r2),
        jnp.where(at == 3, r3, l1),
    ]
    loss, image_acc, text_acc = call(score_kernel, (line, square, square), flops=1 << 30)(*pairs)
    gate = gate_prob.reshape(1, TOK)
    layer_out, image_right = layer_right(tokens, position, gate, returned, head)
    loss, image_acc, text_acc, layer_out, image_right, given = lax.optimization_barrier(
        (loss, image_acc, text_acc, layer_out, image_right, given)
    )
    layer_out, own_image = layer_left(
        tokens, gate, given, head, image_right, labels.reshape(1, PAIRS), layer_out
    )
    own_images = [own_image] + [shift(own_image, step) for step in range(1, LOOP)]
    loss, image_acc = call(own_row_kernel, (line, square), flops=1 << 26, vmem=24)(
        own_image, *pairs, loss, image_acc
    )
    text_acc = call(own_text_kernel, square, flops=1 << 26, vmem=24)(*own_images, own_pairs, text_acc)
    return (layer_out, loss.reshape(PAIRS), image_acc, text_acc)


def solution(mesh):
    fine = Mesh(mesh.devices.reshape(2, 4, 4, 2, LOOP), AXES)
    rows = P(AXES, None)
    flat = P(AXES)
    weights = P(EXPERT, None, "zl")
    in_specs = (rows, rows, flat, P(), weights, weights, rows, P(), rows, flat)
    out_specs = (rows, flat, rows, rows)
    return jax.shard_map(shards, mesh=fine, in_specs=in_specs, out_specs=out_specs, check_vma=False)
```

```python
import functools

import jax
import jax.numpy as jnp
import numpy as np
from jax import lax
from jax.experimental import pallas as pl
from jax.experimental.pallas import tpu as pltpu
from jax.sharding import Mesh
from jax.sharding import PartitionSpec as P

PATCHES = 256
PAIRS = 128
LOOP = 4
RING = 8
PLANE = 32
SLOTS = 6
EXPERTS = 64
GROUPS = 4
PIECE = 48
BLOCK = PLANE * SLOTS
TOK = 256
ROWS = TOK + 16
SHARD = 2 * PAIRS + 16

AXES = ("zh", "y", "x", "c", "zl")
EXPERT = ("zh", "y", "x", "c")
FLAT = ("y", "x", "c")
Z = ("zh", "zl")

scale_logit = 4.0
shift_logit = -1.0

F32 = jnp.float32
BF16 = jnp.bfloat16


def call(kernel, out_shape, scratch=(), aliases=None, flops=0, vmem=60):
    return pl.pallas_call(
        kernel,
        out_shape=out_shape,
        scratch_shapes=list(scratch),
        input_output_aliases=aliases or {},
        cost_estimate=pl.CostEstimate(flops=flops, bytes_accessed=4 << 20, transcendentals=0),
        compiler_params=pltpu.CompilerParams(vmem_limit_bytes=vmem << 20),
    )


def struct(shape, dtype):
    return jax.ShapeDtypeStruct(shape, dtype)


def iota(shape, dim):
    return lax.broadcasted_iota(jnp.int32, shape, dim)


def dot(a, b):
    return jnp.dot(a, b, preferred_element_type=F32)


def dot_t(a, b):
    return lax.dot_general(a, b, (((1,), (1,)), ((), ())), preferred_element_type=F32)


def as_row(column):
    n = column.shape[0]
    return jnp.sum(jnp.where(iota((n, n), 0) == iota((n, n), 1), column, 0.0), 0, keepdims=True)


def as_column(row):
    n = row.shape[1]
    return jnp.sum(jnp.where(iota((n, n), 0) == iota((n, n), 1), row, 0.0), 1, keepdims=True)


def normalize_rows(values):
    return values / jnp.sqrt(jnp.sum(values * values, axis=1, keepdims=True) + 1e-06)


def softplus(x):
    return jnp.maximum(x, 0.0) + jnp.log1p(jnp.exp(-jnp.abs(x)))


def coefficients(logit, sign):
    return (-scale_logit * sign * lax.logistic(-sign * logit)).astype(BF16)


def sign_of(a, b):
    return jnp.where(a == b, 1.0, -1.0)


def swap_matrix():
    order = np.arange(8 * PIECE).reshape(8, 8, SLOTS).transpose(1, 0, 2).reshape(-1)
    return np.eye(8 * PIECE, dtype=np.float32)[order].astype(jnp.bfloat16)


def half_matrix():
    order = np.arange(2 * BLOCK).reshape(PLANE, 2, SLOTS).transpose(1, 0, 2).reshape(-1)
    return np.eye(2 * BLOCK, dtype=np.float32)[order].astype(jnp.bfloat16)


def route_kernel(tokens, routes, quota, packed, outgoing, position):
    half = packed.shape[1]
    ids = as_column(routes[...].astype(F32)).astype(jnp.int32)
    hit = ids == iota((TOK, EXPERTS), 1)
    onehot = jnp.where(hit, 1.0, 0.0)
    before = dot(
        jnp.where(iota((TOK, TOK), 1) < iota((TOK, TOK), 0), 1.0, 0.0).astype(BF16),
        onehot.astype(BF16),
    )
    slot = jnp.sum(onehot * before, axis=1, keepdims=True)
    limit = jnp.sum(onehot * quota[...].astype(F32), axis=1, keepdims=True)
    kept = slot < limit
    far = jnp.where(ids >= PLANE, 1, 0)
    place = (ids - far * PLANE) * (2 * SLOTS) + far * SLOTS
    column = jnp.where(kept, place.astype(F32) + slot, -1.0)
    placing = as_row(column)
    position[...] = placing
    id_row = as_row(ids.astype(F32))
    slot_row = as_row(jnp.where(kept, slot, 64.0))
    line = iota((16, TOK), 0)
    packed[0:TOK, :] = tokens[:, :half]
    packed[TOK:ROWS, :] = jnp.zeros((16, half), BF16)
    packed[TOK:ROWS, 0:TOK] = jnp.where(
        line == 0, id_row, jnp.where(line == 1, slot_row, 0.0)
    ).astype(BF16)
    onto = jnp.where(
        iota((EXPERTS * SLOTS, TOK), 0) == placing.astype(jnp.int32), 1.0, 0.0
    ).astype(BF16)
    outgoing[...] = dot(onto, tokens[:, half:]).astype(BF16)


def choose_kernel(gathered, side, swap, chosen, target, held):
    first = side[0, 0].astype(F32) * PLANE
    for z in range(RING):
        info = gathered[z * ROWS + TOK : (z + 1) * ROWS, 0:TOK].astype(F32)
        ids = info[0:1] - first
        slot = info[1:2]
        mine = (ids >= 0.0) & (ids < float(PLANE)) & (slot < float(SLOTS))
        row = jnp.where(mine, ids * SLOTS + slot, -1.0)
        target[z : z + 1, :] = row
        onto = jnp.where(iota((BLOCK, TOK), 0) == row.astype(jnp.int32), 1.0, 0.0).astype(BF16)
        held[z * BLOCK : (z + 1) * BLOCK, :] = dot(
            onto, gathered[z * ROWS : z * ROWS + TOK, :]
        ).astype(BF16)
    for g in range(GROUPS):
        rows = jnp.concatenate(
            [held[z * BLOCK + g * PIECE : z * BLOCK + (g + 1) * PIECE, :] for z in range(RING)], 0
        )
        chosen[g * 8 * PIECE : (g + 1) * 8 * PIECE, :] = dot(swap[...], rows).astype(BF16)


def spread_kernel(rows, swap, out):
    for g in range(GROUPS):
        moved = dot(swap[...], rows[g * 8 * PIECE : (g + 1) * 8 * PIECE, :]).astype(BF16)
        for z in range(RING):
            at = z * BLOCK + g * PIECE
            out[at : at + PIECE, :] = moved[z * PIECE : (z + 1) * PIECE, :]


def unspread_kernel(rows, swap, out):
    for g in range(GROUPS):
        starts = [z * BLOCK + g * PIECE for z in range(RING)]
        piece = jnp.concatenate([rows[at : at + PIECE, :] for at in starts], 0)
        out[g * 8 * PIECE : (g + 1) * 8 * PIECE, :] = dot(swap[...], piece).astype(BF16)


def turn_kernel(rows, matrix, out):
    out[...] = dot(matrix[...], rows[...]).astype(BF16)


def expert_kernel(side, rows, partial, first, second, hidden, term):
    x = jnp.concatenate([rows[0, 0], rows[1, 0]], 0)
    value = jax.nn.gelu(partial[...] + dot(x, first[...])).astype(BF16)
    hidden[...] = value
    result = dot_t(value, second[...]).astype(BF16)
    nothing = jnp.zeros((BLOCK, result.shape[1]), BF16)
    for k in range(2):
        mine = result[k * BLOCK : (k + 1) * BLOCK]
        for far in range(2):
            term[k, far] = jnp.where(side[0] == far, mine, nothing)


def expert_right(side, rows, partial, first, second):
    half, inner = rows.shape[3], first.shape[1]
    spec = pl.BlockSpec
    return pl.pallas_call(
        expert_kernel,
        out_shape=(
            struct((RING * BLOCK, inner), BF16),
            struct((RING, 2, BLOCK, half), BF16),
        ),
        grid_spec=pltpu.PrefetchScalarGridSpec(
            num_scalar_prefetch=1,
            grid=(RING // 2,),
            in_specs=[
                spec((2, 1, BLOCK, half), lambda i, side: (i, side[0], 0, 0)),
                spec((2 * BLOCK, inner), lambda i, side: (i, 0)),
                spec((half, inner), lambda i, side: (1, 0)),
                spec((half, inner), lambda i, side: (1, 0)),
            ],
            out_specs=[
                spec((2 * BLOCK, inner), lambda i, side: (i, 0)),
                spec((2, 2, BLOCK, half), lambda i, side: (i, 0, 0, 0)),
            ],
        ),
        cost_estimate=pl.CostEstimate(
            flops=4 * RING * BLOCK * half * inner, bytes_accessed=20 << 20, transcendentals=0
        ),
        compiler_params=pltpu.CompilerParams(vmem_limit_bytes=60 << 20),
    )(side, rows, partial, first, second)


def scatter_kernel(rows, swap, target, out, held):
    for g in range(GROUPS):
        moved = dot(swap[...], rows[g * 8 * PIECE : (g + 1) * 8 * PIECE, :]).astype(BF16)
        for z in range(RING):
            at = z * BLOCK + g * PIECE
            held[at : at + PIECE, :] = moved[z * PIECE : (z + 1) * PIECE, :]
    for z in range(RING):
        column = as_column(target[z : z + 1, :]).astype(jnp.int32)
        onto = jnp.where(iota((TOK, BLOCK), 1) == column, 1.0, 0.0).astype(BF16)
        out[z * TOK : (z + 1) * TOK, :] = dot(
            onto, held[z * BLOCK : (z + 1) * BLOCK, :]
        ).astype(BF16)


def own_rows(layer):
    own = (jnp.sum(layer, axis=0, keepdims=True) / PATCHES).astype(BF16)
    return jnp.broadcast_to(own.astype(F32), (16, layer.shape[1])).astype(BF16)


def right_kernel(tokens, position, gate, returned, head, layer_out, image):
    column = as_column(position[...]).astype(jnp.int32)
    onto = jnp.where(iota((TOK, EXPERTS * SLOTS), 1) == column, 1.0, 0.0).astype(BF16)
    weight = as_column(gate[...])
    layer = tokens[...].astype(F32) + weight * dot(onto, returned[...])
    layer_out[...] = layer.astype(BF16)
    image[...] = dot(own_rows(layer), head[...])


def left_kernel(tokens, gate, given, head, partial, label, other_half, layer_out, own_image):
    layer = tokens[...].astype(F32) + as_column(gate[...]) * given[...].astype(F32)
    layer_out[...] = layer.astype(BF16)
    image = normalize_rows(partial[...] + dot(own_rows(layer), head[...]))[0:1]
    embed = image.shape[1]
    own_image[:, :embed] = image.astype(BF16)
    own_image[:, embed:] = label[:, 0:128].astype(F32).astype(BF16)


def whole(shape):
    return pl.BlockSpec(shape, lambda i: (0,) * len(shape))


def part(shape, at):
    return pl.BlockSpec(shape, lambda i: at)


def layer_right(tokens, position, gate, returned, head):
    half, embed = returned.shape[1], head.shape[1]
    return pl.pallas_call(
        right_kernel,
        grid=(1,),
        out_shape=(struct(tokens.shape, BF16), struct((16, embed), F32)),
        in_specs=[
            part((TOK, half), (0, 1)),
            whole((1, TOK)),
            whole((1, TOK)),
            whole(returned.shape),
            part((half, embed), (1, 0)),
        ],
        out_specs=(part((TOK, half), (0, 1)), whole((16, embed))),
        cost_estimate=pl.CostEstimate(flops=1 << 28, bytes_accessed=4 << 20, transcendentals=0),
        compiler_params=pltpu.CompilerParams(vmem_limit_bytes=60 << 20),
    )(tokens, position, gate, returned, head)


def layer_left(tokens, gate, given, head, partial, label, right_done):
    half, embed = given.shape[1], head.shape[1]
    return pl.pallas_call(
        left_kernel,
        grid=(1,),
        out_shape=(struct(tokens.shape, BF16), struct((1, embed + 128), BF16)),
        in_specs=[
            part((TOK, half), (0, 0)),
            whole((1, TOK)),
            whole(given.shape),
            part((half, embed), (0, 0)),
            whole((16, embed)),
            whole(label.shape),
            pl.BlockSpec(memory_space=pl.ANY),
        ],
        out_specs=(part((TOK, half), (0, 0)), whole((1, embed + 128))),
        input_output_aliases={6: 0},
        cost_estimate=pl.CostEstimate(flops=1 << 28, bytes_accessed=4 << 20, transcendentals=0),
        compiler_params=pltpu.CompilerParams(vmem_limit_bytes=60 << 20),
    )(tokens, gate, given, head, partial, label, right_done)


def pack_kernel(pooled, head, text_embed, labels, packed):
    packed[0:PAIRS, :] = normalize_rows(text_embed[...].astype(F32)).astype(BF16)
    image = pltpu.roll(normalize_rows(dot(pooled[...], head[...])), 1, 0)
    image = jnp.where(iota(image.shape, 0) == 0, 0.0, image)
    packed[PAIRS : 2 * PAIRS, :] = image.astype(BF16)
    packed[2 * PAIRS : SHARD, :] = jnp.zeros((16, packed.shape[1]), BF16)
    packed[2 * PAIRS : SHARD, 0:PAIRS] = jnp.where(
        iota((16, PAIRS), 0) == 0, labels[...].astype(F32), 0.0
    ).astype(BF16)


def pack_pairs(pooled, head, text_embed, labels):
    width, embed = head.shape
    return pl.pallas_call(
        pack_kernel,
        grid=(1,),
        out_shape=struct((SHARD, embed), BF16),
        in_specs=[
            whole((PAIRS, width)),
            whole(head.shape),
            whole(text_embed.shape),
            whole(labels.shape),
        ],
        out_specs=whole((SHARD, embed)),
        cost_estimate=pl.CostEstimate(flops=1 << 28, bytes_accessed=4 << 20, transcendentals=0),
        compiler_params=pltpu.CompilerParams(vmem_limit_bytes=60 << 20),
    )(pooled, head, text_embed, labels)


def label_row(shard):
    return shard[2 * PAIRS : SHARD, 0:PAIRS].astype(F32)[0:1]


def score_kernel(own, s1, s2, s3, loss, image_acc, text_acc):
    text = own[0:PAIRS, :]
    image = own[PAIRS : 2 * PAIRS, :]
    mine = as_column(label_row(own))
    losses = jnp.zeros((PAIRS, 1), F32)
    for k, shard in enumerate((own, s1, s2, s3)):
        their_text = shard[0:PAIRS, :]
        their_image = shard[PAIRS : 2 * PAIRS, :]
        sign = sign_of(mine, label_row(shard))
        logit = scale_logit * dot_t(image, their_text) + shift_logit
        losses = losses + jnp.sum(softplus(-sign * logit), axis=1, keepdims=True)
        grad = dot(coefficients(logit, sign), their_text)
        logit = scale_logit * dot_t(text, their_image) + shift_logit
        text_grad = dot(coefficients(logit, sign), their_image)
        image_acc[...] = grad if k == 0 else image_acc[...] + grad
        text_acc[...] = text_grad if k == 0 else text_acc[...] + text_grad
    loss[...] = as_row(losses)


def own_row_kernel(own_image, own, s1, s2, s3, loss, image_acc, loss_out, image_out):
    embed = own.shape[1]
    row = jnp.broadcast_to(own_image[:, :embed].astype(F32), (16, embed)).astype(BF16)
    label = label_row(own)[0:1, 0:1]
    total = jnp.zeros((16, 1), F32)
    grad = jnp.zeros((16, embed), F32)
    for shard in (own, s1, s2, s3):
        their_text = shard[0:PAIRS, :]
        sign = sign_of(label, label_row(shard))
        logit = scale_logit * dot_t(row, their_text) + shift_logit
        total = total + jnp.sum(softplus(-sign * logit), axis=1, keepdims=True)
        grad = grad + dot(coefficients(logit, sign), their_text)
    loss_out[...] = jnp.where(iota((1, PAIRS), 1) == 0, total[0:1], loss[...])
    image_out[...] = image_acc[...]
    image_out[0:1, :] = grad[0:1]


def own_text_kernel(i0, i1, i2, i3, own, text_acc, out):
    embed = own.shape[1]
    line = iota((16, embed), 0)
    place = iota((1, 16), 1)
    images = jnp.zeros((16, embed), F32)
    labels = jnp.full((1, 16), -1.0, F32)
    for k, row in enumerate((i0, i1, i2, i3)):
        images = jnp.where(line == k, row[:, :embed].astype(F32), images)
        labels = jnp.where(place == k, row[:, embed:].astype(F32)[:, 0:1], labels)
    images = images.astype(BF16)
    sign = sign_of(as_column(label_row(own)), labels)
    logit = scale_logit * dot_t(own[0:PAIRS, :], images) + shift_logit
    out[...] = text_acc[...] + dot(coefficients(logit, sign), images)


def shards(
    tokens, routes, gate_prob, expert_quota, w_in, w_out, other_pooled, head, text_embed, labels
):
    width = tokens.shape[1]
    half = width // 2
    embed = head.shape[1]
    swap = jnp.asarray(swap_matrix())
    apart = jnp.asarray(half_matrix())
    together = jnp.asarray(half_matrix().T)
    side = lax.axis_index("zh").astype(jnp.int32).reshape(1, 1)

    packed, outgoing, position = call(
        route_kernel,
        (
            struct((ROWS, half), BF16),
            struct((EXPERTS * SLOTS, half), BF16),
            struct((1, TOK), F32),
        ),
        flops=1 << 28,
    )(tokens, routes.reshape(1, TOK), expert_quota.reshape(1, EXPERTS))

    own_pairs = pack_pairs(other_pooled, head, text_embed, labels.reshape(1, PAIRS))
    shift = lambda value, step: lax.ppermute(
        value, "zl", [(i, (i + step) % LOOP) for i in range(LOOP)]
    )

    outgoing, own_pairs = lax.optimization_barrier((outgoing, own_pairs))

    def onward(right_going, left_going, hops):
        return (
            lax.ppermute(right_going, "zl", [(i, i + 1) for i in range(hops, LOOP - 1)]),
            lax.ppermute(left_going, "zl", [(i, i - 1) for i in range(1, LOOP - hops)]),
        )

    around = lax.all_gather(packed, Z, axis=0, tiled=True)
    received = lax.all_to_all(
        outgoing.reshape(PLANE, 2 * SLOTS, half), FLAT, split_axis=0, concat_axis=0, tiled=True
    ).reshape(2 * BLOCK, half)
    received = call(turn_kernel, struct((2 * BLOCK, half), BF16), flops=1 << 28, vmem=24)(
        received, apart
    )
    r1, l1 = onward(own_pairs, own_pairs, 0)
    received, around, r1, l1 = lax.optimization_barrier((received, around, r1, l1))
    right = lax.all_gather(received, Z, axis=0, tiled=True)

    chosen, target = call(
        choose_kernel,
        (struct((RING * BLOCK, half), BF16), struct((RING, TOK), F32)),
        scratch=[pltpu.VMEM((RING * BLOCK, half), BF16)],
        flops=1 << 30,
        vmem=24,
    )(around, side, swap)
    target, r1, l1 = lax.optimization_barrier((target, r1, l1))
    r2, l2 = onward(r1, l1, 1)
    arrived = lax.all_to_all(
        chosen.reshape(PLANE, PIECE, half), FLAT, split_axis=0, concat_axis=0, tiled=True
    ).reshape(RING * BLOCK, half)
    left = call(spread_kernel, struct((RING * BLOCK, half), BF16), flops=1 << 30, vmem=24)(arrived, swap)

    left, r2, l2 = lax.optimization_barrier((left, r2, l2))
    r3, l3 = onward(r2, l2, 2)

    first = w_in[0]
    second = w_out[0]
    partial = dot(left, first[:half])
    hidden, term_right = expert_right(
        side.reshape(1), right.reshape(RING, 2, BLOCK, half), partial, first, second
    )
    hidden, term_right, r3, l3 = lax.optimization_barrier((hidden, term_right, r3, l3))
    result = lax.psum_scatter(
        term_right.reshape(2 * RING * BLOCK, half), Z, scatter_dimension=0, tiled=True
    )
    term_left = lax.optimization_barrier(dot_t(hidden, second[:half]).astype(BF16))
    leaving = call(unspread_kernel, struct((RING * BLOCK, half), BF16), flops=1 << 30, vmem=24)(
        term_left, swap
    )
    back = lax.all_to_all(
        leaving.reshape(PLANE, PIECE, half), FLAT, split_axis=0, concat_axis=0, tiled=True
    ).reshape(RING * BLOCK, half)
    by_token = call(
        scatter_kernel,
        struct((RING * TOK, half), BF16),
        scratch=[pltpu.VMEM((RING * BLOCK, half), BF16)],
        flops=1 << 30,
    )(back, swap, target)
    by_token, result = lax.optimization_barrier((by_token, result))
    given = lax.psum_scatter(by_token, Z, scatter_dimension=0, tiled=True)
    result = call(turn_kernel, struct((2 * BLOCK, half), BF16), flops=1 << 28, vmem=24)(result, together)
    returned = lax.all_to_all(
        result.reshape(PLANE, 2 * SLOTS, half), FLAT, split_axis=0, concat_axis=0, tiled=True
    ).reshape(2 * BLOCK, half)

    square = struct((PAIRS, embed), F32)
    line = struct((1, PAIRS), F32)
    at = lax.axis_index("zl")
    pairs = [
        own_pairs,
        jnp.where(at == 0, l3, r1),
        jnp.where(at <= 1, l2, r2),
        jnp.where(at == 3, r3, l1),
    ]
    loss, image_acc, text_acc = call(score_kernel, (line, square, square), flops=1 << 30)(*pairs)
    gate = gate_prob.reshape(1, TOK)
    layer_out, image_right = layer_right(tokens, position, gate, returned, head)
    loss, image_acc, text_acc, layer_out, image_right, given = lax.optimization_barrier(
        (loss, image_acc, text_acc, layer_out, image_right, given)
    )
    layer_out, own_image = layer_left(
        tokens, gate, given, head, image_right, labels.reshape(1, PAIRS), layer_out
    )
    own_images = [own_image] + [shift(own_image, step) for step in range(1, LOOP)]
    loss, image_acc = call(own_row_kernel, (line, square), flops=1 << 26, vmem=24)(
        own_image, *pairs, loss, image_acc
    )
    text_acc = call(own_text_kernel, square, flops=1 << 26, vmem=24)(*own_images, own_pairs, text_acc)
    return (layer_out, loss.reshape(PAIRS), image_acc, text_acc)


def solution(mesh):
    fine = Mesh(mesh.devices.reshape(2, 4, 4, 2, LOOP), AXES)
    rows = P(AXES, None)
    flat = P(AXES)
    weights = P(EXPERT, None, "zl")
    in_specs = (rows, rows, flat, P(), weights, weights, rows, P(), rows, flat)
    out_specs = (rows, flat, rows, rows)
    return jax.shard_map(shards, mesh=fine, in_specs=in_specs, out_specs=out_specs, check_vma=False)
```

```python
import functools

import jax
import jax.numpy as jnp
import numpy as np
from jax import lax
from jax.experimental import pallas as pl
from jax.experimental.pallas import tpu as pltpu
from jax.sharding import Mesh
from jax.sharding import PartitionSpec as P

PATCHES = 256
PAIRS = 128
LOOP = 4
RING = 8
PLANE = 32
SLOTS = 6
EXPERTS = 64
GROUPS = 4
PIECE = 48
BLOCK = PLANE * SLOTS
TOK = 256
ROWS = TOK + 16
SHARD = 2 * PAIRS + 16

AXES = ("zh", "y", "x", "c", "zl")
EXPERT = ("zh", "y", "x", "c")
FLAT = ("y", "x", "c")
Z = ("zh", "zl")

scale_logit = 4.0
shift_logit = -1.0

F32 = jnp.float32
BF16 = jnp.bfloat16


def call(kernel, out_shape, scratch=(), aliases=None, flops=0, vmem=60):
    return pl.pallas_call(
        kernel,
        out_shape=out_shape,
        scratch_shapes=list(scratch),
        input_output_aliases=aliases or {},
        cost_estimate=pl.CostEstimate(flops=flops, bytes_accessed=4 << 20, transcendentals=0),
        compiler_params=pltpu.CompilerParams(vmem_limit_bytes=vmem << 20),
    )


def struct(shape, dtype):
    return jax.ShapeDtypeStruct(shape, dtype)


def iota(shape, dim):
    return lax.broadcasted_iota(jnp.int32, shape, dim)


def dot(a, b):
    return jnp.dot(a, b, preferred_element_type=F32)


def dot_t(a, b):
    return lax.dot_general(a, b, (((1,), (1,)), ((), ())), preferred_element_type=F32)


def as_row(column):
    n = column.shape[0]
    return jnp.sum(jnp.where(iota((n, n), 0) == iota((n, n), 1), column, 0.0), 0, keepdims=True)


def as_column(row):
    n = row.shape[1]
    return jnp.sum(jnp.where(iota((n, n), 0) == iota((n, n), 1), row, 0.0), 1, keepdims=True)


def normalize_rows(values):
    return values / jnp.sqrt(jnp.sum(values * values, axis=1, keepdims=True) + 1e-06)


def softplus(x):
    return jnp.maximum(x, 0.0) + jnp.log1p(jnp.exp(-jnp.abs(x)))


def coefficients(logit, sign):
    return (-scale_logit * sign * lax.logistic(-sign * logit)).astype(BF16)


def sign_of(a, b):
    return jnp.where(a == b, 1.0, -1.0)


def swap_matrix():
    order = np.arange(8 * PIECE).reshape(8, 8, SLOTS).transpose(1, 0, 2).reshape(-1)
    return np.eye(8 * PIECE, dtype=np.float32)[order].astype(jnp.bfloat16)


def half_matrix():
    order = np.arange(2 * BLOCK).reshape(PLANE, 2, SLOTS).transpose(1, 0, 2).reshape(-1)
    return np.eye(2 * BLOCK, dtype=np.float32)[order].astype(jnp.bfloat16)


def route_kernel(tokens, routes, quota, packed, outgoing, position):
    half = packed.shape[1]
    ids = as_column(routes[...].astype(F32)).astype(jnp.int32)
    hit = ids == iota((TOK, EXPERTS), 1)
    onehot = jnp.where(hit, 1.0, 0.0)
    before = dot(
        jnp.where(iota((TOK, TOK), 1) < iota((TOK, TOK), 0), 1.0, 0.0).astype(BF16),
        onehot.astype(BF16),
    )
    slot = jnp.sum(onehot * before, axis=1, keepdims=True)
    limit = jnp.sum(onehot * quota[...].astype(F32), axis=1, keepdims=True)
    kept = slot < limit
    far = jnp.where(ids >= PLANE, 1, 0)
    place = (ids - far * PLANE) * (2 * SLOTS) + far * SLOTS
    column = jnp.where(kept, place.astype(F32) + slot, -1.0)
    placing = as_row(column)
    position[...] = placing
    id_row = as_row(ids.astype(F32))
    slot_row = as_row(jnp.where(kept, slot, 64.0))
    line = iota((16, TOK), 0)
    packed[0:TOK, :] = tokens[:, :half]
    packed[TOK:ROWS, :] = jnp.zeros((16, half), BF16)
    packed[TOK:ROWS, 0:TOK] = jnp.where(
        line == 0, id_row, jnp.where(line == 1, slot_row, 0.0)
    ).astype(BF16)
    onto = jnp.where(
        iota((EXPERTS * SLOTS, TOK), 0) == placing.astype(jnp.int32), 1.0, 0.0
    ).astype(BF16)
    outgoing[...] = dot(onto, tokens[:, half:]).astype(BF16)


def choose_kernel(gathered, side, swap, chosen, target, held):
    first = side[0, 0].astype(F32) * PLANE
    for z in range(RING):
        info = gathered[z * ROWS + TOK : (z + 1) * ROWS, 0:TOK].astype(F32)
        ids = info[0:1] - first
        slot = info[1:2]
        mine = (ids >= 0.0) & (ids < float(PLANE)) & (slot < float(SLOTS))
        row = jnp.where(mine, ids * SLOTS + slot, -1.0)
        target[z : z + 1, :] = row
        onto = jnp.where(iota((BLOCK, TOK), 0) == row.astype(jnp.int32), 1.0, 0.0).astype(BF16)
        held[z * BLOCK : (z + 1) * BLOCK, :] = dot(
            onto, gathered[z * ROWS : z * ROWS + TOK, :]
        ).astype(BF16)
    for g in range(GROUPS):
        rows = jnp.concatenate(
            [held[z * BLOCK + g * PIECE : z * BLOCK + (g + 1) * PIECE, :] for z in range(RING)], 0
        )
        chosen[g * 8 * PIECE : (g + 1) * 8 * PIECE, :] = dot(swap[...], rows).astype(BF16)


def spread_kernel(rows, swap, out):
    for g in range(GROUPS):
        moved = dot(swap[...], rows[g * 8 * PIECE : (g + 1) * 8 * PIECE, :]).astype(BF16)
        for z in range(RING):
            at = z * BLOCK + g * PIECE
            out[at : at + PIECE, :] = moved[z * PIECE : (z + 1) * PIECE, :]


def unspread_kernel(rows, swap, out):
    for g in range(GROUPS):
        starts = [z * BLOCK + g * PIECE for z in range(RING)]
        piece = jnp.concatenate([rows[at : at + PIECE, :] for at in starts], 0)
        out[g * 8 * PIECE : (g + 1) * 8 * PIECE, :] = dot(swap[...], piece).astype(BF16)


def turn_kernel(rows, matrix, out):
    out[...] = dot(matrix[...], rows[...]).astype(BF16)


def expert_kernel(side, rows, partial, first, second, hidden, term):
    x = jnp.concatenate([rows[0, 0], rows[1, 0]], 0)
    value = jax.nn.gelu(partial[...] + dot(x, first[...])).astype(BF16)
    hidden[...] = value
    result = dot_t(value, second[...]).astype(BF16)
    nothing = jnp.zeros((BLOCK, result.shape[1]), BF16)
    for k in range(2):
        mine = result[k * BLOCK : (k + 1) * BLOCK]
        for far in range(2):
            term[k, far] = jnp.where(side[0] == far, mine, nothing)


def expert_right(side, rows, partial, first, second):
    half, inner = rows.shape[3], first.shape[1]
    spec = pl.BlockSpec
    return pl.pallas_call(
        expert_kernel,
        out_shape=(
            struct((RING * BLOCK, inner), BF16),
            struct((RING, 2, BLOCK, half), BF16),
        ),
        grid_spec=pltpu.PrefetchScalarGridSpec(
            num_scalar_prefetch=1,
            grid=(RING // 2,),
            in_specs=[
                spec((2, 1, BLOCK, half), lambda i, side: (i, side[0], 0, 0)),
                spec((2 * BLOCK, inner), lambda i, side: (i, 0)),
                spec((half, inner), lambda i, side: (1, 0)),
                spec((half, inner), lambda i, side: (1, 0)),
            ],
            out_specs=[
                spec((2 * BLOCK, inner), lambda i, side: (i, 0)),
                spec((2, 2, BLOCK, half), lambda i, side: (i, 0, 0, 0)),
            ],
        ),
        cost_estimate=pl.CostEstimate(
            flops=4 * RING * BLOCK * half * inner, bytes_accessed=20 << 20, transcendentals=0
        ),
        compiler_params=pltpu.CompilerParams(vmem_limit_bytes=60 << 20),
    )(side, rows, partial, first, second)


def scatter_kernel(rows, swap, target, out, held):
    for g in range(GROUPS):
        moved = dot(swap[...], rows[g * 8 * PIECE : (g + 1) * 8 * PIECE, :]).astype(BF16)
        for z in range(RING):
            at = z * BLOCK + g * PIECE
            held[at : at + PIECE, :] = moved[z * PIECE : (z + 1) * PIECE, :]
    for z in range(RING):
        column = as_column(target[z : z + 1, :]).astype(jnp.int32)
        onto = jnp.where(iota((TOK, BLOCK), 1) == column, 1.0, 0.0).astype(BF16)
        out[z * TOK : (z + 1) * TOK, :] = dot(
            onto, held[z * BLOCK : (z + 1) * BLOCK, :]
        ).astype(BF16)


def own_rows(layer):
    own = (jnp.sum(layer, axis=0, keepdims=True) / PATCHES).astype(BF16)
    return jnp.broadcast_to(own.astype(F32), (16, layer.shape[1])).astype(BF16)


def right_kernel(tokens, position, gate, returned, head, layer_out, image):
    column = as_column(position[...]).astype(jnp.int32)
    onto = jnp.where(iota((TOK, EXPERTS * SLOTS), 1) == column, 1.0, 0.0).astype(BF16)
    weight = as_column(gate[...])
    layer = tokens[...].astype(F32) + weight * dot(onto, returned[...])
    layer_out[...] = layer.astype(BF16)
    image[...] = dot(own_rows(layer), head[...])


def left_kernel(tokens, gate, given, head, partial, label, other_half, layer_out, own_image):
    layer = tokens[...].astype(F32) + as_column(gate[...]) * given[...].astype(F32)
    layer_out[...] = layer.astype(BF16)
    image = normalize_rows(partial[...] + dot(own_rows(layer), head[...]))[0:1]
    embed = image.shape[1]
    own_image[:, :embed] = image.astype(BF16)
    own_image[:, embed:] = label[:, 0:128].astype(F32).astype(BF16)


def whole(shape):
    return pl.BlockSpec(shape, lambda i: (0,) * len(shape))


def part(shape, at):
    return pl.BlockSpec(shape, lambda i: at)


def layer_right(tokens, position, gate, returned, head):
    half, embed = returned.shape[1], head.shape[1]
    return pl.pallas_call(
        right_kernel,
        grid=(1,),
        out_shape=(struct(tokens.shape, BF16), struct((16, embed), F32)),
        in_specs=[
            part((TOK, half), (0, 1)),
            whole((1, TOK)),
            whole((1, TOK)),
            whole(returned.shape),
            part((half, embed), (1, 0)),
        ],
        out_specs=(part((TOK, half), (0, 1)), whole((16, embed))),
        cost_estimate=pl.CostEstimate(flops=1 << 28, bytes_accessed=4 << 20, transcendentals=0),
        compiler_params=pltpu.CompilerParams(vmem_limit_bytes=60 << 20),
    )(tokens, position, gate, returned, head)


def layer_left(tokens, gate, given, head, partial, label, right_done):
    half, embed = given.shape[1], head.shape[1]
    return pl.pallas_call(
        left_kernel,
        grid=(1,),
        out_shape=(struct(tokens.shape, BF16), struct((1, embed + 128), BF16)),
        in_specs=[
            part((TOK, half), (0, 0)),
            whole((1, TOK)),
            whole(given.shape),
            part((half, embed), (0, 0)),
            whole((16, embed)),
            whole(label.shape),
            pl.BlockSpec(memory_space=pl.ANY),
        ],
        out_specs=(part((TOK, half), (0, 0)), whole((1, embed + 128))),
        input_output_aliases={6: 0},
        cost_estimate=pl.CostEstimate(flops=1 << 28, bytes_accessed=4 << 20, transcendentals=0),
        compiler_params=pltpu.CompilerParams(vmem_limit_bytes=60 << 20),
    )(tokens, gate, given, head, partial, label, right_done)


def pack_kernel(pooled, head, text_embed, labels, packed):
    packed[0:PAIRS, :] = normalize_rows(text_embed[...].astype(F32)).astype(BF16)
    image = pltpu.roll(normalize_rows(dot(pooled[...], head[...])), 1, 0)
    image = jnp.where(iota(image.shape, 0) == 0, 0.0, image)
    packed[PAIRS : 2 * PAIRS, :] = image.astype(BF16)
    packed[2 * PAIRS : SHARD, :] = jnp.zeros((16, packed.shape[1]), BF16)
    packed[2 * PAIRS : SHARD, 0:PAIRS] = jnp.where(
        iota((16, PAIRS), 0) == 0, labels[...].astype(F32), 0.0
    ).astype(BF16)


def pack_pairs(pooled, head, text_embed, labels):
    width, embed = head.shape
    return pl.pallas_call(
        pack_kernel,
        grid=(1,),
        out_shape=struct((SHARD, embed), BF16),
        in_specs=[
            whole((PAIRS, width)),
            whole(head.shape),
            whole(text_embed.shape),
            whole(labels.shape),
        ],
        out_specs=whole((SHARD, embed)),
        cost_estimate=pl.CostEstimate(flops=1 << 28, bytes_accessed=4 << 20, transcendentals=0),
        compiler_params=pltpu.CompilerParams(vmem_limit_bytes=60 << 20),
    )(pooled, head, text_embed, labels)


def label_row(shard):
    return shard[2 * PAIRS : SHARD, 0:PAIRS].astype(F32)[0:1]


def score_kernel(own, s1, s2, s3, loss, image_acc, text_acc):
    text = own[0:PAIRS, :]
    image = own[PAIRS : 2 * PAIRS, :]
    mine = as_column(label_row(own))
    losses = jnp.zeros((PAIRS, 1), F32)
    for k, shard in enumerate((own, s1, s2, s3)):
        their_text = shard[0:PAIRS, :]
        their_image = shard[PAIRS : 2 * PAIRS, :]
        sign = sign_of(mine, label_row(shard))
        logit = scale_logit * dot_t(image, their_text) + shift_logit
        losses = losses + jnp.sum(softplus(-sign * logit), axis=1, keepdims=True)
        grad = dot(coefficients(logit, sign), their_text)
        logit = scale_logit * dot_t(text, their_image) + shift_logit
        text_grad = dot(coefficients(logit, sign), their_image)
        image_acc[...] = grad if k == 0 else image_acc[...] + grad
        text_acc[...] = text_grad if k == 0 else text_acc[...] + text_grad
    loss[...] = as_row(losses)


def own_row_kernel(own_image, own, s1, s2, s3, loss, image_acc, loss_out, image_out):
    embed = own.shape[1]
    row = jnp.broadcast_to(own_image[:, :embed].astype(F32), (16, embed)).astype(BF16)
    label = label_row(own)[0:1, 0:1]
    total = jnp.zeros((16, 1), F32)
    grad = jnp.zeros((16, embed), F32)
    for shard in (own, s1, s2, s3):
        their_text = shard[0:PAIRS, :]
        sign = sign_of(label, label_row(shard))
        logit = scale_logit * dot_t(row, their_text) + shift_logit
        total = total + jnp.sum(softplus(-sign * logit), axis=1, keepdims=True)
        grad = grad + dot(coefficients(logit, sign), their_text)
    loss_out[...] = jnp.where(iota((1, PAIRS), 1) == 0, total[0:1], loss[...])
    image_out[...] = image_acc[...]
    image_out[0:1, :] = grad[0:1]


def own_text_kernel(i0, i1, i2, i3, own, text_acc, out):
    embed = own.shape[1]
    line = iota((16, embed), 0)
    place = iota((1, 16), 1)
    images = jnp.zeros((16, embed), F32)
    labels = jnp.full((1, 16), -1.0, F32)
    for k, row in enumerate((i0, i1, i2, i3)):
        images = jnp.where(line == k, row[:, :embed].astype(F32), images)
        labels = jnp.where(place == k, row[:, embed:].astype(F32)[:, 0:1], labels)
    images = images.astype(BF16)
    sign = sign_of(as_column(label_row(own)), labels)
    logit = scale_logit * dot_t(own[0:PAIRS, :], images) + shift_logit
    out[...] = text_acc[...] + dot(coefficients(logit, sign), images)


def shards(
    tokens, routes, gate_prob, expert_quota, w_in, w_out, other_pooled, head, text_embed, labels
):
    width = tokens.shape[1]
    half = width // 2
    embed = head.shape[1]
    swap = jnp.asarray(swap_matrix())
    apart = jnp.asarray(half_matrix())
    together = jnp.asarray(half_matrix().T)
    side = lax.axis_index("zh").astype(jnp.int32).reshape(1, 1)

    packed, outgoing, position = call(
        route_kernel,
        (
            struct((ROWS, half), BF16),
            struct((EXPERTS * SLOTS, half), BF16),
            struct((1, TOK), F32),
        ),
        flops=1 << 28,
    )(tokens, routes.reshape(1, TOK), expert_quota.reshape(1, EXPERTS))

    own_pairs = pack_pairs(other_pooled, head, text_embed, labels.reshape(1, PAIRS))
    shift = lambda value, step: lax.ppermute(
        value, "zl", [(i, (i + step) % LOOP) for i in range(LOOP)]
    )


    def both(right_going, left_going, senders, hops):
        return (
            lax.ppermute(right_going, "zl", [(i, i + hops) for i in senders]),
            lax.ppermute(left_going, "zl", [(LOOP - 1 - i, LOOP - 1 - i - hops) for i in senders]),
        )

    around = lax.all_gather(packed, Z, axis=0, tiled=True)
    received = lax.all_to_all(
        outgoing.reshape(PLANE, 2 * SLOTS, half), FLAT, split_axis=0, concat_axis=0, tiled=True
    ).reshape(2 * BLOCK, half)
    received = call(turn_kernel, struct((2 * BLOCK, half), BF16), flops=1 << 28, vmem=24)(
        received, apart
    )
    received, around, own_pairs = lax.optimization_barrier((received, around, own_pairs))
    right = lax.all_gather(received, Z, axis=0, tiled=True)

    chosen, target = call(
        choose_kernel,
        (struct((RING * BLOCK, half), BF16), struct((RING, TOK), F32)),
        scratch=[pltpu.VMEM((RING * BLOCK, half), BF16)],
        flops=1 << 30,
    )(around, side, swap)
    arrived = lax.all_to_all(
        chosen.reshape(PLANE, PIECE, half), FLAT, split_axis=0, concat_axis=0, tiled=True
    ).reshape(RING * BLOCK, half)
    left = call(spread_kernel, struct((RING * BLOCK, half), BF16), flops=1 << 30, vmem=24)(arrived, swap)


    first = w_in[0]
    second = w_out[0]
    partial = dot(left, first[:half])
    partial, own_pairs = lax.optimization_barrier((partial, own_pairs))
    r1, l1 = both(own_pairs, own_pairs, (0, 1, 2), 1)
    hidden, term_right = expert_right(
        side.reshape(1), right.reshape(RING, 2, BLOCK, half), partial, first, second
    )
    hidden, term_right, r1, l1 = lax.optimization_barrier((hidden, term_right, r1, l1))
    result = lax.psum_scatter(
        term_right.reshape(2 * RING * BLOCK, half), Z, scatter_dimension=0, tiled=True
    )
    term_left = lax.optimization_barrier(dot_t(hidden, second[:half]).astype(BF16))
    leaving = call(unspread_kernel, struct((RING * BLOCK, half), BF16), flops=1 << 30, vmem=24)(
        term_left, swap
    )
    back = lax.all_to_all(
        leaving.reshape(PLANE, PIECE, half), FLAT, split_axis=0, concat_axis=0, tiled=True
    ).reshape(RING * BLOCK, half)
    by_token = call(
        scatter_kernel,
        struct((RING * TOK, half), BF16),
        scratch=[pltpu.VMEM((RING * BLOCK, half), BF16)],
        flops=1 << 30,
    )(back, swap, target)
    by_token, result, r1, l1, own_pairs = lax.optimization_barrier(
        (by_token, result, r1, l1, own_pairs)
    )
    r2, l2 = both(r1, l1, (1, 2), 1)
    r3, l3 = both(own_pairs, own_pairs, (0,), 3)
    given = lax.psum_scatter(by_token, Z, scatter_dimension=0, tiled=True)
    result = call(turn_kernel, struct((2 * BLOCK, half), BF16), flops=1 << 28, vmem=24)(result, together)
    returned = lax.all_to_all(
        result.reshape(PLANE, 2 * SLOTS, half), FLAT, split_axis=0, concat_axis=0, tiled=True
    ).reshape(2 * BLOCK, half)

    square = struct((PAIRS, embed), F32)
    line = struct((1, PAIRS), F32)
    at = lax.axis_index("zl")
    pairs = [
        own_pairs,
        jnp.where(at == 0, l3, r1),
        jnp.where(at <= 1, l2, r2),
        jnp.where(at == 3, r3, l1),
    ]
    loss, image_acc, text_acc = call(score_kernel, (line, square, square), flops=1 << 30)(*pairs)
    gate = gate_prob.reshape(1, TOK)
    layer_out, image_right = layer_right(tokens, position, gate, returned, head)
    loss, image_acc, text_acc, layer_out, image_right, given = lax.optimization_barrier(
        (loss, image_acc, text_acc, layer_out, image_right, given)
    )
    layer_out, own_image = layer_left(
        tokens, gate, given, head, image_right, labels.reshape(1, PAIRS), layer_out
    )
    own_images = [own_image] + [shift(own_image, step) for step in range(1, LOOP)]
    loss, image_acc = call(own_row_kernel, (line, square), flops=1 << 26, vmem=24)(
        own_image, *pairs, loss, image_acc
    )
    text_acc = call(own_text_kernel, square, flops=1 << 26, vmem=24)(*own_images, own_pairs, text_acc)
    return (layer_out, loss.reshape(PAIRS), image_acc, text_acc)


def solution(mesh):
    fine = Mesh(mesh.devices.reshape(2, 4, 4, 2, LOOP), AXES)
    rows = P(AXES, None)
    flat = P(AXES)
    weights = P(EXPERT, None, "zl")
    in_specs = (rows, rows, flat, P(), weights, weights, rows, P(), rows, flat)
    out_specs = (rows, flat, rows, rows)
    return jax.shard_map(shards, mesh=fine, in_specs=in_specs, out_specs=out_specs, check_vma=False)
```

```python
import functools

import jax
import jax.numpy as jnp
import numpy as np
from jax import lax
from jax.experimental import pallas as pl
from jax.experimental.pallas import tpu as pltpu
from jax.sharding import Mesh
from jax.sharding import PartitionSpec as P

PATCHES = 256
PAIRS = 128
LOOP = 4
RING = 8
PLANE = 32
SLOTS = 6
EXPERTS = 64
GROUPS = 4
PIECE = 48
BLOCK = PLANE * SLOTS
TOK = 256
ROWS = TOK + 16
SHARD = 2 * PAIRS + 16

AXES = ("zh", "y", "x", "c", "zl")
EXPERT = ("zh", "y", "x", "c")
FLAT = ("y", "x", "c")
Z = ("zh", "zl")

scale_logit = 4.0
shift_logit = -1.0

F32 = jnp.float32
BF16 = jnp.bfloat16


def call(kernel, out_shape, scratch=(), aliases=None, flops=0, vmem=60):
    return pl.pallas_call(
        kernel,
        out_shape=out_shape,
        scratch_shapes=list(scratch),
        input_output_aliases=aliases or {},
        cost_estimate=pl.CostEstimate(flops=flops, bytes_accessed=4 << 20, transcendentals=0),
        compiler_params=pltpu.CompilerParams(vmem_limit_bytes=vmem << 20),
    )


def struct(shape, dtype):
    return jax.ShapeDtypeStruct(shape, dtype)


def iota(shape, dim):
    return lax.broadcasted_iota(jnp.int32, shape, dim)


def dot(a, b):
    return jnp.dot(a, b, preferred_element_type=F32)


def dot_t(a, b):
    return lax.dot_general(a, b, (((1,), (1,)), ((), ())), preferred_element_type=F32)


def as_row(column):
    n = column.shape[0]
    return jnp.sum(jnp.where(iota((n, n), 0) == iota((n, n), 1), column, 0.0), 0, keepdims=True)


def as_column(row):
    n = row.shape[1]
    return jnp.sum(jnp.where(iota((n, n), 0) == iota((n, n), 1), row, 0.0), 1, keepdims=True)


def normalize_rows(values):
    return values / jnp.sqrt(jnp.sum(values * values, axis=1, keepdims=True) + 1e-06)


def softplus(x):
    return jnp.maximum(x, 0.0) + jnp.log1p(jnp.exp(-jnp.abs(x)))


def coefficients(logit, sign):
    return (-scale_logit * sign * lax.logistic(-sign * logit)).astype(BF16)


def sign_of(a, b):
    return jnp.where(a == b, 1.0, -1.0)


def swap_matrix():
    order = np.arange(8 * PIECE).reshape(8, 8, SLOTS).transpose(1, 0, 2).reshape(-1)
    return np.eye(8 * PIECE, dtype=np.float32)[order].astype(jnp.bfloat16)


def half_matrix():
    order = np.arange(2 * BLOCK).reshape(PLANE, 2, SLOTS).transpose(1, 0, 2).reshape(-1)
    return np.eye(2 * BLOCK, dtype=np.float32)[order].astype(jnp.bfloat16)


def route_kernel(tokens, routes, quota, packed, outgoing, position):
    half = packed.shape[1]
    ids = as_column(routes[...].astype(F32)).astype(jnp.int32)
    hit = ids == iota((TOK, EXPERTS), 1)
    onehot = jnp.where(hit, 1.0, 0.0)
    before = dot(
        jnp.where(iota((TOK, TOK), 1) < iota((TOK, TOK), 0), 1.0, 0.0).astype(BF16),
        onehot.astype(BF16),
    )
    slot = jnp.sum(onehot * before, axis=1, keepdims=True)
    limit = jnp.sum(onehot * quota[...].astype(F32), axis=1, keepdims=True)
    kept = slot < limit
    far = jnp.where(ids >= PLANE, 1, 0)
    place = (ids - far * PLANE) * (2 * SLOTS) + far * SLOTS
    column = jnp.where(kept, place.astype(F32) + slot, -1.0)
    placing = as_row(column)
    position[...] = placing
    id_row = as_row(ids.astype(F32))
    slot_row = as_row(jnp.where(kept, slot, 64.0))
    line = iota((16, TOK), 0)
    packed[0:TOK, :] = tokens[:, :half]
    packed[TOK:ROWS, :] = jnp.zeros((16, half), BF16)
    packed[TOK:ROWS, 0:TOK] = jnp.where(
        line == 0, id_row, jnp.where(line == 1, slot_row, 0.0)
    ).astype(BF16)
    onto = jnp.where(
        iota((EXPERTS * SLOTS, TOK), 0) == placing.astype(jnp.int32), 1.0, 0.0
    ).astype(BF16)
    outgoing[...] = dot(onto, tokens[:, half:]).astype(BF16)


def choose_kernel(gathered, side, swap, chosen, target, held):
    first = side[0, 0].astype(F32) * PLANE
    for z in range(RING):
        info = gathered[z * ROWS + TOK : (z + 1) * ROWS, 0:TOK].astype(F32)
        ids = info[0:1] - first
        slot = info[1:2]
        mine = (ids >= 0.0) & (ids < float(PLANE)) & (slot < float(SLOTS))
        row = jnp.where(mine, ids * SLOTS + slot, -1.0)
        target[z : z + 1, :] = row
        onto = jnp.where(iota((BLOCK, TOK), 0) == row.astype(jnp.int32), 1.0, 0.0).astype(BF16)
        held[z * BLOCK : (z + 1) * BLOCK, :] = dot(
            onto, gathered[z * ROWS : z * ROWS + TOK, :]
        ).astype(BF16)
    for g in range(GROUPS):
        rows = jnp.concatenate(
            [held[z * BLOCK + g * PIECE : z * BLOCK + (g + 1) * PIECE, :] for z in range(RING)], 0
        )
        chosen[g * 8 * PIECE : (g + 1) * 8 * PIECE, :] = dot(swap[...], rows).astype(BF16)


def spread_kernel(rows, swap, out):
    for g in range(GROUPS):
        moved = dot(swap[...], rows[g * 8 * PIECE : (g + 1) * 8 * PIECE, :]).astype(BF16)
        for z in range(RING):
            at = z * BLOCK + g * PIECE
            out[at : at + PIECE, :] = moved[z * PIECE : (z + 1) * PIECE, :]


def unspread_kernel(rows, swap, out):
    for g in range(GROUPS):
        starts = [z * BLOCK + g * PIECE for z in range(RING)]
        piece = jnp.concatenate([rows[at : at + PIECE, :] for at in starts], 0)
        out[g * 8 * PIECE : (g + 1) * 8 * PIECE, :] = dot(swap[...], piece).astype(BF16)


def turn_kernel(rows, matrix, out):
    out[...] = dot(matrix[...], rows[...]).astype(BF16)


def expert_kernel(side, rows, partial, first, second, hidden, term):
    x = jnp.concatenate([rows[0, 0], rows[1, 0]], 0)
    value = jax.nn.gelu(partial[...] + dot(x, first[...])).astype(BF16)
    hidden[...] = value
    result = dot_t(value, second[...]).astype(BF16)
    nothing = jnp.zeros((BLOCK, result.shape[1]), BF16)
    for k in range(2):
        mine = result[k * BLOCK : (k + 1) * BLOCK]
        for far in range(2):
            term[k, far] = jnp.where(side[0] == far, mine, nothing)


def expert_right(side, rows, partial, first, second):
    half, inner = rows.shape[3], first.shape[1]
    spec = pl.BlockSpec
    return pl.pallas_call(
        expert_kernel,
        out_shape=(
            struct((RING * BLOCK, inner), BF16),
            struct((RING, 2, BLOCK, half), BF16),
        ),
        grid_spec=pltpu.PrefetchScalarGridSpec(
            num_scalar_prefetch=1,
            grid=(RING // 2,),
            in_specs=[
                spec((2, 1, BLOCK, half), lambda i, side: (i, side[0], 0, 0)),
                spec((2 * BLOCK, inner), lambda i, side: (i, 0)),
                spec((half, inner), lambda i, side: (1, 0)),
                spec((half, inner), lambda i, side: (1, 0)),
            ],
            out_specs=[
                spec((2 * BLOCK, inner), lambda i, side: (i, 0)),
                spec((2, 2, BLOCK, half), lambda i, side: (i, 0, 0, 0)),
            ],
        ),
        cost_estimate=pl.CostEstimate(
            flops=4 * RING * BLOCK * half * inner, bytes_accessed=20 << 20, transcendentals=0
        ),
        compiler_params=pltpu.CompilerParams(vmem_limit_bytes=60 << 20),
    )(side, rows, partial, first, second)


def scatter_kernel(rows, swap, target, out, held):
    for g in range(GROUPS):
        moved = dot(swap[...], rows[g * 8 * PIECE : (g + 1) * 8 * PIECE, :]).astype(BF16)
        for z in range(RING):
            at = z * BLOCK + g * PIECE
            held[at : at + PIECE, :] = moved[z * PIECE : (z + 1) * PIECE, :]
    for z in range(RING):
        column = as_column(target[z : z + 1, :]).astype(jnp.int32)
        onto = jnp.where(iota((TOK, BLOCK), 1) == column, 1.0, 0.0).astype(BF16)
        out[z * TOK : (z + 1) * TOK, :] = dot(
            onto, held[z * BLOCK : (z + 1) * BLOCK, :]
        ).astype(BF16)


def own_rows(layer):
    own = (jnp.sum(layer, axis=0, keepdims=True) / PATCHES).astype(BF16)
    return jnp.broadcast_to(own.astype(F32), (16, layer.shape[1])).astype(BF16)


def right_kernel(tokens, position, gate, returned, head, layer_out, image):
    column = as_column(position[...]).astype(jnp.int32)
    onto = jnp.where(iota((TOK, EXPERTS * SLOTS), 1) == column, 1.0, 0.0).astype(BF16)
    weight = as_column(gate[...])
    layer = tokens[...].astype(F32) + weight * dot(onto, returned[...])
    layer_out[...] = layer.astype(BF16)
    image[...] = dot(own_rows(layer), head[...])


def left_kernel(tokens, gate, given, head, partial, label, other_half, layer_out, own_image):
    layer = tokens[...].astype(F32) + as_column(gate[...]) * given[...].astype(F32)
    layer_out[...] = layer.astype(BF16)
    image = normalize_rows(partial[...] + dot(own_rows(layer), head[...]))[0:1]
    embed = image.shape[1]
    own_image[:, :embed] = image.astype(BF16)
    own_image[:, embed:] = label[:, 0:128].astype(F32).astype(BF16)


def whole(shape):
    return pl.BlockSpec(shape, lambda i: (0,) * len(shape))


def part(shape, at):
    return pl.BlockSpec(shape, lambda i: at)


def layer_right(tokens, position, gate, returned, head):
    half, embed = returned.shape[1], head.shape[1]
    return pl.pallas_call(
        right_kernel,
        grid=(1,),
        out_shape=(struct(tokens.shape, BF16), struct((16, embed), F32)),
        in_specs=[
            part((TOK, half), (0, 1)),
            whole((1, TOK)),
            whole((1, TOK)),
            whole(returned.shape),
            part((half, embed), (1, 0)),
        ],
        out_specs=(part((TOK, half), (0, 1)), whole((16, embed))),
        cost_estimate=pl.CostEstimate(flops=1 << 28, bytes_accessed=4 << 20, transcendentals=0),
        compiler_params=pltpu.CompilerParams(vmem_limit_bytes=60 << 20),
    )(tokens, position, gate, returned, head)


def layer_left(tokens, gate, given, head, partial, label, right_done):
    half, embed = given.shape[1], head.shape[1]
    return pl.pallas_call(
        left_kernel,
        grid=(1,),
        out_shape=(struct(tokens.shape, BF16), struct((1, embed + 128), BF16)),
        in_specs=[
            part((TOK, half), (0, 0)),
            whole((1, TOK)),
            whole(given.shape),
            part((half, embed), (0, 0)),
            whole((16, embed)),
            whole(label.shape),
            pl.BlockSpec(memory_space=pl.ANY),
        ],
        out_specs=(part((TOK, half), (0, 0)), whole((1, embed + 128))),
        input_output_aliases={6: 0},
        cost_estimate=pl.CostEstimate(flops=1 << 28, bytes_accessed=4 << 20, transcendentals=0),
        compiler_params=pltpu.CompilerParams(vmem_limit_bytes=60 << 20),
    )(tokens, gate, given, head, partial, label, right_done)


def pack_kernel(pooled, head, text_embed, labels, packed):
    packed[0:PAIRS, :] = normalize_rows(text_embed[...].astype(F32)).astype(BF16)
    image = pltpu.roll(normalize_rows(dot(pooled[...], head[...])), 1, 0)
    image = jnp.where(iota(image.shape, 0) == 0, 0.0, image)
    packed[PAIRS : 2 * PAIRS, :] = image.astype(BF16)
    packed[2 * PAIRS : SHARD, :] = jnp.zeros((16, packed.shape[1]), BF16)
    packed[2 * PAIRS : SHARD, 0:PAIRS] = jnp.where(
        iota((16, PAIRS), 0) == 0, labels[...].astype(F32), 0.0
    ).astype(BF16)


def pack_pairs(pooled, head, text_embed, labels):
    width, embed = head.shape
    return pl.pallas_call(
        pack_kernel,
        grid=(1,),
        out_shape=struct((SHARD, embed), BF16),
        in_specs=[
            whole((PAIRS, width)),
            whole(head.shape),
            whole(text_embed.shape),
            whole(labels.shape),
        ],
        out_specs=whole((SHARD, embed)),
        cost_estimate=pl.CostEstimate(flops=1 << 28, bytes_accessed=4 << 20, transcendentals=0),
        compiler_params=pltpu.CompilerParams(vmem_limit_bytes=60 << 20),
    )(pooled, head, text_embed, labels)


def label_row(shard):
    return shard[2 * PAIRS : SHARD, 0:PAIRS].astype(F32)[0:1]


def score_kernel(own, s1, s2, s3, loss, image_acc, text_acc):
    text = own[0:PAIRS, :]
    image = own[PAIRS : 2 * PAIRS, :]
    mine = as_column(label_row(own))
    losses = jnp.zeros((PAIRS, 1), F32)
    for k, shard in enumerate((own, s1, s2, s3)):
        their_text = shard[0:PAIRS, :]
        their_image = shard[PAIRS : 2 * PAIRS, :]
        sign = sign_of(mine, label_row(shard))
        logit = scale_logit * dot_t(image, their_text) + shift_logit
        losses = losses + jnp.sum(softplus(-sign * logit), axis=1, keepdims=True)
        grad = dot(coefficients(logit, sign), their_text)
        logit = scale_logit * dot_t(text, their_image) + shift_logit
        text_grad = dot(coefficients(logit, sign), their_image)
        image_acc[...] = grad if k == 0 else image_acc[...] + grad
        text_acc[...] = text_grad if k == 0 else text_acc[...] + text_grad
    loss[...] = as_row(losses)


def own_row_kernel(own_image, own, s1, s2, s3, loss, image_acc, loss_out, image_out):
    embed = own.shape[1]
    row = jnp.broadcast_to(own_image[:, :embed].astype(F32), (16, embed)).astype(BF16)
    label = label_row(own)[0:1, 0:1]
    total = jnp.zeros((16, 1), F32)
    grad = jnp.zeros((16, embed), F32)
    for shard in (own, s1, s2, s3):
        their_text = shard[0:PAIRS, :]
        sign = sign_of(label, label_row(shard))
        logit = scale_logit * dot_t(row, their_text) + shift_logit
        total = total + jnp.sum(softplus(-sign * logit), axis=1, keepdims=True)
        grad = grad + dot(coefficients(logit, sign), their_text)
    loss_out[...] = jnp.where(iota((1, PAIRS), 1) == 0, total[0:1], loss[...])
    image_out[...] = image_acc[...]
    image_out[0:1, :] = grad[0:1]


def own_text_kernel(i0, i1, i2, i3, own, text_acc, out):
    embed = own.shape[1]
    line = iota((16, embed), 0)
    place = iota((1, 16), 1)
    images = jnp.zeros((16, embed), F32)
    labels = jnp.full((1, 16), -1.0, F32)
    for k, row in enumerate((i0, i1, i2, i3)):
        images = jnp.where(line == k, row[:, :embed].astype(F32), images)
        labels = jnp.where(place == k, row[:, embed:].astype(F32)[:, 0:1], labels)
    images = images.astype(BF16)
    sign = sign_of(as_column(label_row(own)), labels)
    logit = scale_logit * dot_t(own[0:PAIRS, :], images) + shift_logit
    out[...] = text_acc[...] + dot(coefficients(logit, sign), images)


def shards(
    tokens, routes, gate_prob, expert_quota, w_in, w_out, other_pooled, head, text_embed, labels
):
    width = tokens.shape[1]
    half = width // 2
    embed = head.shape[1]
    swap = jnp.asarray(swap_matrix())
    apart = jnp.asarray(half_matrix())
    together = jnp.asarray(half_matrix().T)
    side = lax.axis_index("zh").astype(jnp.int32).reshape(1, 1)

    packed, outgoing, position = call(
        route_kernel,
        (
            struct((ROWS, half), BF16),
            struct((EXPERTS * SLOTS, half), BF16),
            struct((1, TOK), F32),
        ),
        flops=1 << 28,
    )(tokens, routes.reshape(1, TOK), expert_quota.reshape(1, EXPERTS))

    own_pairs = pack_pairs(other_pooled, head, text_embed, labels.reshape(1, PAIRS))
    shift = lambda value, step: lax.ppermute(
        value, "zl", [(i, (i + step) % LOOP) for i in range(LOOP)]
    )


    def both(right_going, left_going, senders, hops):
        return (
            lax.ppermute(right_going, "zl", [(i, i + hops) for i in senders]),
            lax.ppermute(left_going, "zl", [(LOOP - 1 - i, LOOP - 1 - i - hops) for i in senders]),
        )

    around = lax.all_gather(packed, Z, axis=0, tiled=True)
    received = lax.all_to_all(
        outgoing.reshape(PLANE, 2 * SLOTS, half), FLAT, split_axis=0, concat_axis=0, tiled=True
    ).reshape(2 * BLOCK, half)
    received = call(turn_kernel, struct((2 * BLOCK, half), BF16), flops=1 << 28, vmem=24)(
        received, apart
    )
    received, around, own_pairs = lax.optimization_barrier((received, around, own_pairs))
    right = lax.all_gather(received, Z, axis=0, tiled=True)

    chosen, target = call(
        choose_kernel,
        (struct((RING * BLOCK, half), BF16), struct((RING, TOK), F32)),
        scratch=[pltpu.VMEM((RING * BLOCK, half), BF16)],
        flops=1 << 30,
    )(around, side, swap)
    arrived = lax.all_to_all(
        chosen.reshape(PLANE, PIECE, half), FLAT, split_axis=0, concat_axis=0, tiled=True
    ).reshape(RING * BLOCK, half)
    left = call(spread_kernel, struct((RING * BLOCK, half), BF16), flops=1 << 30, vmem=24)(arrived, swap)


    first = w_in[0]
    second = w_out[0]
    partial = dot(left, first[:half])
    partial, own_pairs = lax.optimization_barrier((partial, own_pairs))
    r1, l1 = both(own_pairs, own_pairs, (0, 1, 2), 1)
    hidden, term_right = expert_right(
        side.reshape(1), right.reshape(RING, 2, BLOCK, half), partial, first, second
    )
    hidden, term_right, r1, l1 = lax.optimization_barrier((hidden, term_right, r1, l1))
    result = lax.psum_scatter(
        term_right.reshape(2 * RING * BLOCK, half), Z, scatter_dimension=0, tiled=True
    )
    term_left = lax.optimization_barrier(dot_t(hidden, second[:half]).astype(BF16))
    leaving = call(unspread_kernel, struct((RING * BLOCK, half), BF16), flops=1 << 30, vmem=24)(
        term_left, swap
    )
    back = lax.all_to_all(
        leaving.reshape(PLANE, PIECE, half), FLAT, split_axis=0, concat_axis=0, tiled=True
    ).reshape(RING * BLOCK, half)
    by_token = call(
        scatter_kernel,
        struct((RING * TOK, half), BF16),
        scratch=[pltpu.VMEM((RING * BLOCK, half), BF16)],
        flops=1 << 30,
    )(back, swap, target)
    by_token, result, r1, l1, own_pairs = lax.optimization_barrier(
        (by_token, result, r1, l1, own_pairs)
    )
    r2, l2 = both(r1, l1, (1, 2), 1)
    r3, l3 = both(own_pairs, own_pairs, (0,), 3)
    given = lax.psum_scatter(by_token, Z, scatter_dimension=0, tiled=True)
    result = call(turn_kernel, struct((2 * BLOCK, half), BF16), flops=1 << 28, vmem=24)(result, together)
    returned = lax.all_to_all(
        result.reshape(PLANE, 2 * SLOTS, half), FLAT, split_axis=0, concat_axis=0, tiled=True
    ).reshape(2 * BLOCK, half)

    returned, r2, l2, r3, l3 = lax.optimization_barrier((returned, r2, l2, r3, l3))

    square = struct((PAIRS, embed), F32)
    line = struct((1, PAIRS), F32)
    at = lax.axis_index("zl")
    pairs = [
        own_pairs,
        jnp.where(at == 0, l3, r1),
        jnp.where(at <= 1, l2, r2),
        jnp.where(at == 3, r3, l1),
    ]
    loss, image_acc, text_acc = call(score_kernel, (line, square, square), flops=1 << 30)(*pairs)
    gate = gate_prob.reshape(1, TOK)
    layer_out, image_right = layer_right(tokens, position, gate, returned, head)
    loss, image_acc, text_acc, layer_out, image_right, given = lax.optimization_barrier(
        (loss, image_acc, text_acc, layer_out, image_right, given)
    )
    layer_out, own_image = layer_left(
        tokens, gate, given, head, image_right, labels.reshape(1, PAIRS), layer_out
    )
    own_images = [own_image] + [shift(own_image, step) for step in range(1, LOOP)]
    loss, image_acc = call(own_row_kernel, (line, square), flops=1 << 26, vmem=24)(
        own_image, *pairs, loss, image_acc
    )
    text_acc = call(own_text_kernel, square, flops=1 << 26, vmem=24)(*own_images, own_pairs, text_acc)
    return (layer_out, loss.reshape(PAIRS), image_acc, text_acc)


def solution(mesh):
    fine = Mesh(mesh.devices.reshape(2, 4, 4, 2, LOOP), AXES)
    rows = P(AXES, None)
    flat = P(AXES)
    weights = P(EXPERT, None, "zl")
    in_specs = (rows, rows, flat, P(), weights, weights, rows, P(), rows, flat)
    out_specs = (rows, flat, rows, rows)
    return jax.shard_map(shards, mesh=fine, in_specs=in_specs, out_specs=out_specs, check_vma=False)
```

```python
import functools

import jax
import jax.numpy as jnp
import numpy as np
from jax import lax
from jax.experimental import pallas as pl
from jax.experimental.pallas import tpu as pltpu
from jax.sharding import Mesh
from jax.sharding import PartitionSpec as P

PATCHES = 256
PAIRS = 128
LOOP = 4
RING = 8
PLANE = 32
SLOTS = 6
EXPERTS = 64
GROUPS = 4
PIECE = 48
BLOCK = PLANE * SLOTS
TOK = 256
ROWS = TOK + 16
SHARD = 2 * PAIRS + 16

AXES = ("zh", "y", "x", "c", "zl")
EXPERT = ("zh", "y", "x", "c")
FLAT = ("y", "x", "c")
Z = ("zh", "zl")

scale_logit = 4.0
shift_logit = -1.0

F32 = jnp.float32
BF16 = jnp.bfloat16


def call(kernel, out_shape, scratch=(), aliases=None, flops=0, vmem=60):
    return pl.pallas_call(
        kernel,
        out_shape=out_shape,
        scratch_shapes=list(scratch),
        input_output_aliases=aliases or {},
        cost_estimate=pl.CostEstimate(flops=flops, bytes_accessed=4 << 20, transcendentals=0),
        compiler_params=pltpu.CompilerParams(vmem_limit_bytes=vmem << 20),
    )


def struct(shape, dtype):
    return jax.ShapeDtypeStruct(shape, dtype)


def iota(shape, dim):
    return lax.broadcasted_iota(jnp.int32, shape, dim)


def dot(a, b):
    return jnp.dot(a, b, preferred_element_type=F32)


def dot_t(a, b):
    return lax.dot_general(a, b, (((1,), (1,)), ((), ())), preferred_element_type=F32)


def as_row(column):
    n = column.shape[0]
    return jnp.sum(jnp.where(iota((n, n), 0) == iota((n, n), 1), column, 0.0), 0, keepdims=True)


def as_column(row):
    n = row.shape[1]
    return jnp.sum(jnp.where(iota((n, n), 0) == iota((n, n), 1), row, 0.0), 1, keepdims=True)


def normalize_rows(values):
    return values / jnp.sqrt(jnp.sum(values * values, axis=1, keepdims=True) + 1e-06)


def softplus(x):
    return jnp.maximum(x, 0.0) + jnp.log1p(jnp.exp(-jnp.abs(x)))


def coefficients(logit, sign):
    return (-scale_logit * sign * lax.logistic(-sign * logit)).astype(BF16)


def sign_of(a, b):
    return jnp.where(a == b, 1.0, -1.0)


def swap_matrix():
    order = np.arange(8 * PIECE).reshape(8, 8, SLOTS).transpose(1, 0, 2).reshape(-1)
    return np.eye(8 * PIECE, dtype=np.float32)[order].astype(jnp.bfloat16)


def half_matrix():
    order = np.arange(2 * BLOCK).reshape(PLANE, 2, SLOTS).transpose(1, 0, 2).reshape(-1)
    return np.eye(2 * BLOCK, dtype=np.float32)[order].astype(jnp.bfloat16)


def route_kernel(tokens, routes, quota, packed, outgoing, position):
    half = packed.shape[1]
    ids = as_column(routes[...].astype(F32)).astype(jnp.int32)
    hit = ids == iota((TOK, EXPERTS), 1)
    onehot = jnp.where(hit, 1.0, 0.0)
    before = dot(
        jnp.where(iota((TOK, TOK), 1) < iota((TOK, TOK), 0), 1.0, 0.0).astype(BF16),
        onehot.astype(BF16),
    )
    slot = jnp.sum(onehot * before, axis=1, keepdims=True)
    limit = jnp.sum(onehot * quota[...].astype(F32), axis=1, keepdims=True)
    kept = slot < limit
    far = jnp.where(ids >= PLANE, 1, 0)
    place = (ids - far * PLANE) * (2 * SLOTS) + far * SLOTS
    column = jnp.where(kept, place.astype(F32) + slot, -1.0)
    placing = as_row(column)
    position[...] = placing
    id_row = as_row(ids.astype(F32))
    slot_row = as_row(jnp.where(kept, slot, 64.0))
    line = iota((16, TOK), 0)
    packed[0:TOK, :] = tokens[:, :half]
    packed[TOK:ROWS, :] = jnp.zeros((16, half), BF16)
    packed[TOK:ROWS, 0:TOK] = jnp.where(
        line == 0, id_row, jnp.where(line == 1, slot_row, 0.0)
    ).astype(BF16)
    onto = jnp.where(
        iota((EXPERTS * SLOTS, TOK), 0) == placing.astype(jnp.int32), 1.0, 0.0
    ).astype(BF16)
    outgoing[...] = dot(onto, tokens[:, half:]).astype(BF16)


def choose_kernel(gathered, side, swap, chosen, target, held):
    first = side[0, 0].astype(F32) * PLANE
    for z in range(RING):
        info = gathered[z * ROWS + TOK : (z + 1) * ROWS, 0:TOK].astype(F32)
        ids = info[0:1] - first
        slot = info[1:2]
        mine = (ids >= 0.0) & (ids < float(PLANE)) & (slot < float(SLOTS))
        row = jnp.where(mine, ids * SLOTS + slot, -1.0)
        target[z : z + 1, :] = row
        onto = jnp.where(iota((BLOCK, TOK), 0) == row.astype(jnp.int32), 1.0, 0.0).astype(BF16)
        held[z * BLOCK : (z + 1) * BLOCK, :] = dot(
            onto, gathered[z * ROWS : z * ROWS + TOK, :]
        ).astype(BF16)
    for g in range(GROUPS):
        rows = jnp.concatenate(
            [held[z * BLOCK + g * PIECE : z * BLOCK + (g + 1) * PIECE, :] for z in range(RING)], 0
        )
        chosen[g * 8 * PIECE : (g + 1) * 8 * PIECE, :] = dot(swap[...], rows).astype(BF16)


def spread_kernel(rows, swap, out):
    for g in range(GROUPS):
        moved = dot(swap[...], rows[g * 8 * PIECE : (g + 1) * 8 * PIECE, :]).astype(BF16)
        for z in range(RING):
            at = z * BLOCK + g * PIECE
            out[at : at + PIECE, :] = moved[z * PIECE : (z + 1) * PIECE, :]


def unspread_kernel(rows, swap, out):
    for g in range(GROUPS):
        starts = [z * BLOCK + g * PIECE for z in range(RING)]
        piece = jnp.concatenate([rows[at : at + PIECE, :] for at in starts], 0)
        out[g * 8 * PIECE : (g + 1) * 8 * PIECE, :] = dot(swap[...], piece).astype(BF16)


def turn_kernel(rows, matrix, out):
    out[...] = dot(matrix[...], rows[...]).astype(BF16)


def expert_kernel(side, rows, partial, first, second, hidden, term):
    x = jnp.concatenate([rows[0, 0], rows[1, 0]], 0)
    value = jax.nn.gelu(partial[...] + dot(x, first[...])).astype(BF16)
    hidden[...] = value
    result = dot_t(value, second[...]).astype(BF16)
    nothing = jnp.zeros((BLOCK, result.shape[1]), BF16)
    for k in range(2):
        mine = result[k * BLOCK : (k + 1) * BLOCK]
        for far in range(2):
            term[k, far] = jnp.where(side[0] == far, mine, nothing)


def expert_right(side, rows, partial, first, second):
    half, inner = rows.shape[3], first.shape[1]
    spec = pl.BlockSpec
    return pl.pallas_call(
        expert_kernel,
        out_shape=(
            struct((RING * BLOCK, inner), BF16),
            struct((RING, 2, BLOCK, half), BF16),
        ),
        grid_spec=pltpu.PrefetchScalarGridSpec(
            num_scalar_prefetch=1,
            grid=(RING // 2,),
            in_specs=[
                spec((2, 1, BLOCK, half), lambda i, side: (i, side[0], 0, 0)),
                spec((2 * BLOCK, inner), lambda i, side: (i, 0)),
                spec((half, inner), lambda i, side: (1, 0)),
                spec((half, inner), lambda i, side: (1, 0)),
            ],
            out_specs=[
                spec((2 * BLOCK, inner), lambda i, side: (i, 0)),
                spec((2, 2, BLOCK, half), lambda i, side: (i, 0, 0, 0)),
            ],
        ),
        cost_estimate=pl.CostEstimate(
            flops=4 * RING * BLOCK * half * inner, bytes_accessed=20 << 20, transcendentals=0
        ),
        compiler_params=pltpu.CompilerParams(vmem_limit_bytes=60 << 20),
    )(side, rows, partial, first, second)


def scatter_kernel(rows, swap, target, out, held):
    for g in range(GROUPS):
        moved = dot(swap[...], rows[g * 8 * PIECE : (g + 1) * 8 * PIECE, :]).astype(BF16)
        for z in range(RING):
            at = z * BLOCK + g * PIECE
            held[at : at + PIECE, :] = moved[z * PIECE : (z + 1) * PIECE, :]
    for z in range(RING):
        column = as_column(target[z : z + 1, :]).astype(jnp.int32)
        onto = jnp.where(iota((TOK, BLOCK), 1) == column, 1.0, 0.0).astype(BF16)
        out[z * TOK : (z + 1) * TOK, :] = dot(
            onto, held[z * BLOCK : (z + 1) * BLOCK, :]
        ).astype(BF16)


def own_rows(layer):
    own = (jnp.sum(layer, axis=0, keepdims=True) / PATCHES).astype(BF16)
    return jnp.broadcast_to(own.astype(F32), (16, layer.shape[1])).astype(BF16)


def right_kernel(tokens, position, gate, returned, head, layer_out, image):
    column = as_column(position[...]).astype(jnp.int32)
    onto = jnp.where(iota((TOK, EXPERTS * SLOTS), 1) == column, 1.0, 0.0).astype(BF16)
    weight = as_column(gate[...])
    layer = tokens[...].astype(F32) + weight * dot(onto, returned[...])
    layer_out[...] = layer.astype(BF16)
    image[...] = dot(own_rows(layer), head[...])


def left_kernel(tokens, gate, given, head, partial, label, other_half, layer_out, own_image):
    layer = tokens[...].astype(F32) + as_column(gate[...]) * given[...].astype(F32)
    layer_out[...] = layer.astype(BF16)
    image = normalize_rows(partial[...] + dot(own_rows(layer), head[...]))[0:1]
    embed = image.shape[1]
    own_image[:, :embed] = image.astype(BF16)
    own_image[:, embed:] = label[:, 0:128].astype(F32).astype(BF16)


def whole(shape):
    return pl.BlockSpec(shape, lambda i: (0,) * len(shape))


def part(shape, at):
    return pl.BlockSpec(shape, lambda i: at)


def layer_right(tokens, position, gate, returned, head):
    half, embed = returned.shape[1], head.shape[1]
    return pl.pallas_call(
        right_kernel,
        grid=(1,),
        out_shape=(struct(tokens.shape, BF16), struct((16, embed), F32)),
        in_specs=[
            part((TOK, half), (0, 1)),
            whole((1, TOK)),
            whole((1, TOK)),
            whole(returned.shape),
            part((half, embed), (1, 0)),
        ],
        out_specs=(part((TOK, half), (0, 1)), whole((16, embed))),
        cost_estimate=pl.CostEstimate(flops=1 << 28, bytes_accessed=4 << 20, transcendentals=0),
        compiler_params=pltpu.CompilerParams(vmem_limit_bytes=60 << 20),
    )(tokens, position, gate, returned, head)


def layer_left(tokens, gate, given, head, partial, label, right_done):
    half, embed = given.shape[1], head.shape[1]
    return pl.pallas_call(
        left_kernel,
        grid=(1,),
        out_shape=(struct(tokens.shape, BF16), struct((1, embed + 128), BF16)),
        in_specs=[
            part((TOK, half), (0, 0)),
            whole((1, TOK)),
            whole(given.shape),
            part((half, embed), (0, 0)),
            whole((16, embed)),
            whole(label.shape),
            pl.BlockSpec(memory_space=pl.ANY),
        ],
        out_specs=(part((TOK, half), (0, 0)), whole((1, embed + 128))),
        input_output_aliases={6: 0},
        cost_estimate=pl.CostEstimate(flops=1 << 28, bytes_accessed=4 << 20, transcendentals=0),
        compiler_params=pltpu.CompilerParams(vmem_limit_bytes=60 << 20),
    )(tokens, gate, given, head, partial, label, right_done)


def pack_kernel(pooled, head, text_embed, labels, packed):
    packed[0:PAIRS, :] = normalize_rows(text_embed[...].astype(F32)).astype(BF16)
    image = pltpu.roll(normalize_rows(dot(pooled[...], head[...])), 1, 0)
    image = jnp.where(iota(image.shape, 0) == 0, 0.0, image)
    packed[PAIRS : 2 * PAIRS, :] = image.astype(BF16)
    packed[2 * PAIRS : SHARD, :] = jnp.zeros((16, packed.shape[1]), BF16)
    packed[2 * PAIRS : SHARD, 0:PAIRS] = jnp.where(
        iota((16, PAIRS), 0) == 0, labels[...].astype(F32), 0.0
    ).astype(BF16)


def pack_pairs(pooled, head, text_embed, labels):
    width, embed = head.shape
    return pl.pallas_call(
        pack_kernel,
        grid=(1,),
        out_shape=struct((SHARD, embed), BF16),
        in_specs=[
            whole((PAIRS, width)),
            whole(head.shape),
            whole(text_embed.shape),
            whole(labels.shape),
        ],
        out_specs=whole((SHARD, embed)),
        cost_estimate=pl.CostEstimate(flops=1 << 28, bytes_accessed=4 << 20, transcendentals=0),
        compiler_params=pltpu.CompilerParams(vmem_limit_bytes=60 << 20),
    )(pooled, head, text_embed, labels)


def label_row(shard):
    return shard[2 * PAIRS : SHARD, 0:PAIRS].astype(F32)[0:1]


def score_kernel(own, s1, s2, s3, loss, image_acc, text_acc):
    text = own[0:PAIRS, :]
    image = own[PAIRS : 2 * PAIRS, :]
    mine = as_column(label_row(own))
    losses = jnp.zeros((PAIRS, 1), F32)
    for k, shard in enumerate((own, s1, s2, s3)):
        their_text = shard[0:PAIRS, :]
        their_image = shard[PAIRS : 2 * PAIRS, :]
        sign = sign_of(mine, label_row(shard))
        logit = scale_logit * dot_t(image, their_text) + shift_logit
        losses = losses + jnp.sum(softplus(-sign * logit), axis=1, keepdims=True)
        grad = dot(coefficients(logit, sign), their_text)
        logit = scale_logit * dot_t(text, their_image) + shift_logit
        text_grad = dot(coefficients(logit, sign), their_image)
        image_acc[...] = grad if k == 0 else image_acc[...] + grad
        text_acc[...] = text_grad if k == 0 else text_acc[...] + text_grad
    loss[...] = as_row(losses)


def own_row_kernel(own_image, own, s1, s2, s3, loss, image_acc, loss_out, image_out):
    embed = own.shape[1]
    row = jnp.broadcast_to(own_image[:, :embed].astype(F32), (16, embed)).astype(BF16)
    label = label_row(own)[0:1, 0:1]
    total = jnp.zeros((16, 1), F32)
    grad = jnp.zeros((16, embed), F32)
    for shard in (own, s1, s2, s3):
        their_text = shard[0:PAIRS, :]
        sign = sign_of(label, label_row(shard))
        logit = scale_logit * dot_t(row, their_text) + shift_logit
        total = total + jnp.sum(softplus(-sign * logit), axis=1, keepdims=True)
        grad = grad + dot(coefficients(logit, sign), their_text)
    loss_out[...] = jnp.where(iota((1, PAIRS), 1) == 0, total[0:1], loss[...])
    image_out[...] = image_acc[...]
    image_out[0:1, :] = grad[0:1]


def own_text_kernel(i0, i1, i2, i3, own, text_acc, out):
    embed = own.shape[1]
    line = iota((16, embed), 0)
    place = iota((1, 16), 1)
    images = jnp.zeros((16, embed), F32)
    labels = jnp.full((1, 16), -1.0, F32)
    for k, row in enumerate((i0, i1, i2, i3)):
        images = jnp.where(line == k, row[:, :embed].astype(F32), images)
        labels = jnp.where(place == k, row[:, embed:].astype(F32)[:, 0:1], labels)
    images = images.astype(BF16)
    sign = sign_of(as_column(label_row(own)), labels)
    logit = scale_logit * dot_t(own[0:PAIRS, :], images) + shift_logit
    out[...] = text_acc[...] + dot(coefficients(logit, sign), images)


def shards(
    tokens, routes, gate_prob, expert_quota, w_in, w_out, other_pooled, head, text_embed, labels
):
    width = tokens.shape[1]
    half = width // 2
    embed = head.shape[1]
    swap = jnp.asarray(swap_matrix())
    apart = jnp.asarray(half_matrix())
    together = jnp.asarray(half_matrix().T)
    side = lax.axis_index("zh").astype(jnp.int32).reshape(1, 1)

    packed, outgoing, position = call(
        route_kernel,
        (
            struct((ROWS, half), BF16),
            struct((EXPERTS * SLOTS, half), BF16),
            struct((1, TOK), F32),
        ),
        flops=1 << 28,
    )(tokens, routes.reshape(1, TOK), expert_quota.reshape(1, EXPERTS))

    own_pairs = pack_pairs(other_pooled, head, text_embed, labels.reshape(1, PAIRS))
    shift = lambda value, step: lax.ppermute(
        value, "zl", [(i, (i + step) % LOOP) for i in range(LOOP)]
    )


    def both(right_going, left_going, senders, hops):
        return (
            lax.ppermute(right_going, "zl", [(i, i + hops) for i in senders]),
            lax.ppermute(left_going, "zl", [(LOOP - 1 - i, LOOP - 1 - i - hops) for i in senders]),
        )

    around = lax.all_gather(packed, Z, axis=0, tiled=True)
    received = lax.all_to_all(
        outgoing.reshape(PLANE, 2 * SLOTS, half), FLAT, split_axis=0, concat_axis=0, tiled=True
    ).reshape(2 * BLOCK, half)
    received = call(turn_kernel, struct((2 * BLOCK, half), BF16), flops=1 << 28, vmem=24)(
        received, apart
    )
    received, around, own_pairs = lax.optimization_barrier((received, around, own_pairs))
    right = lax.all_gather(received, Z, axis=0, tiled=True)

    chosen, target = call(
        choose_kernel,
        (struct((RING * BLOCK, half), BF16), struct((RING, TOK), F32)),
        scratch=[pltpu.VMEM((RING * BLOCK, half), BF16)],
        flops=1 << 30,
    )(around, side, swap)
    arrived = lax.all_to_all(
        chosen.reshape(PLANE, PIECE, half), FLAT, split_axis=0, concat_axis=0, tiled=True
    ).reshape(RING * BLOCK, half)
    left = call(spread_kernel, struct((RING * BLOCK, half), BF16), flops=1 << 30, vmem=24)(arrived, swap)


    first = w_in[0]
    second = w_out[0]
    partial = dot(left, first[:half])
    partial, own_pairs = lax.optimization_barrier((partial, own_pairs))
    r1, l1 = both(own_pairs, own_pairs, (0, 1, 2), 1)
    hidden, term_right = expert_right(
        side.reshape(1), right.reshape(RING, 2, BLOCK, half), partial, first, second
    )
    hidden, term_right, r1, l1 = lax.optimization_barrier((hidden, term_right, r1, l1))
    right_texts, left_texts = both(r1[:PAIRS], l1[:PAIRS], (1, 2), 1)
    result = lax.psum_scatter(
        term_right.reshape(2 * RING * BLOCK, half), Z, scatter_dimension=0, tiled=True
    )
    term_left = lax.optimization_barrier(dot_t(hidden, second[:half]).astype(BF16))
    leaving = call(unspread_kernel, struct((RING * BLOCK, half), BF16), flops=1 << 30, vmem=24)(
        term_left, swap
    )
    leaving, right_texts, left_texts = lax.optimization_barrier(
        (leaving, right_texts, left_texts)
    )
    back = lax.all_to_all(
        leaving.reshape(PLANE, PIECE, half), FLAT, split_axis=0, concat_axis=0, tiled=True
    ).reshape(RING * BLOCK, half)
    by_token = call(
        scatter_kernel,
        struct((RING * TOK, half), BF16),
        scratch=[pltpu.VMEM((RING * BLOCK, half), BF16)],
        flops=1 << 30,
    )(back, swap, target)
    by_token, result, right_rest, left_rest, own_pairs = lax.optimization_barrier(
        (by_token, result, r1[PAIRS:], l1[PAIRS:], own_pairs)
    )
    r2, l2 = both(right_rest, left_rest, (1, 2), 1)
    r3, l3 = both(own_pairs, own_pairs, (0,), 3)
    given = lax.psum_scatter(by_token, Z, scatter_dimension=0, tiled=True)
    result = call(turn_kernel, struct((2 * BLOCK, half), BF16), flops=1 << 28, vmem=24)(result, together)
    returned = lax.all_to_all(
        result.reshape(PLANE, 2 * SLOTS, half), FLAT, split_axis=0, concat_axis=0, tiled=True
    ).reshape(2 * BLOCK, half)

    returned, r2, l2, r3, l3 = lax.optimization_barrier((returned, r2, l2, r3, l3))
    r2 = jnp.concatenate([right_texts, r2], axis=0)
    l2 = jnp.concatenate([left_texts, l2], axis=0)

    square = struct((PAIRS, embed), F32)
    line = struct((1, PAIRS), F32)
    at = lax.axis_index("zl")
    pairs = [
        own_pairs,
        jnp.where(at == 0, l3, r1),
        jnp.where(at <= 1, l2, r2),
        jnp.where(at == 3, r3, l1),
    ]
    loss, image_acc, text_acc = call(score_kernel, (line, square, square), flops=1 << 30)(*pairs)
    gate = gate_prob.reshape(1, TOK)
    layer_out, image_right = layer_right(tokens, position, gate, returned, head)
    loss, image_acc, text_acc, layer_out, image_right, given = lax.optimization_barrier(
        (loss, image_acc, text_acc, layer_out, image_right, given)
    )
    layer_out, own_image = layer_left(
        tokens, gate, given, head, image_right, labels.reshape(1, PAIRS), layer_out
    )
    own_images = [own_image] + [shift(own_image, step) for step in range(1, LOOP)]
    loss, image_acc = call(own_row_kernel, (line, square), flops=1 << 26, vmem=24)(
        own_image, *pairs, loss, image_acc
    )
    text_acc = call(own_text_kernel, square, flops=1 << 26, vmem=24)(*own_images, own_pairs, text_acc)
    return (layer_out, loss.reshape(PAIRS), image_acc, text_acc)


def solution(mesh):
    fine = Mesh(mesh.devices.reshape(2, 4, 4, 2, LOOP), AXES)
    rows = P(AXES, None)
    flat = P(AXES)
    weights = P(EXPERT, None, "zl")
    in_specs = (rows, rows, flat, P(), weights, weights, rows, P(), rows, flat)
    out_specs = (rows, flat, rows, rows)
    return jax.shard_map(shards, mesh=fine, in_specs=in_specs, out_specs=out_specs, check_vma=False)
```

```python
import functools

import jax
import jax.numpy as jnp
import numpy as np
from jax import lax
from jax.experimental import pallas as pl
from jax.experimental.pallas import tpu as pltpu
from jax.sharding import Mesh
from jax.sharding import PartitionSpec as P

PATCHES = 256
PAIRS = 128
LOOP = 4
RING = 8
PLANE = 32
SLOTS = 6
EXPERTS = 64
GROUPS = 4
PIECE = 48
BLOCK = PLANE * SLOTS
TOK = 256
ROWS = TOK + 16
SHARD = 2 * PAIRS + 16

AXES = ("zh", "y", "x", "c", "zl")
EXPERT = ("zh", "y", "x", "c")
FLAT = ("y", "x", "c")
Z = ("zh", "zl")

scale_logit = 4.0
shift_logit = -1.0

F32 = jnp.float32
BF16 = jnp.bfloat16


def call(kernel, out_shape, scratch=(), aliases=None, flops=0, vmem=60):
    return pl.pallas_call(
        kernel,
        out_shape=out_shape,
        scratch_shapes=list(scratch),
        input_output_aliases=aliases or {},
        cost_estimate=pl.CostEstimate(flops=flops, bytes_accessed=4 << 20, transcendentals=0),
        compiler_params=pltpu.CompilerParams(vmem_limit_bytes=vmem << 20),
    )


def struct(shape, dtype):
    return jax.ShapeDtypeStruct(shape, dtype)


def iota(shape, dim):
    return lax.broadcasted_iota(jnp.int32, shape, dim)


def dot(a, b):
    return jnp.dot(a, b, preferred_element_type=F32)


def dot_t(a, b):
    return lax.dot_general(a, b, (((1,), (1,)), ((), ())), preferred_element_type=F32)


def as_row(column):
    n = column.shape[0]
    return jnp.sum(jnp.where(iota((n, n), 0) == iota((n, n), 1), column, 0.0), 0, keepdims=True)


def as_column(row):
    n = row.shape[1]
    return jnp.sum(jnp.where(iota((n, n), 0) == iota((n, n), 1), row, 0.0), 1, keepdims=True)


def normalize_rows(values):
    return values / jnp.sqrt(jnp.sum(values * values, axis=1, keepdims=True) + 1e-06)


def softplus(x):
    return jnp.maximum(x, 0.0) + jnp.log1p(jnp.exp(-jnp.abs(x)))


def coefficients(logit, sign):
    return (-scale_logit * sign * lax.logistic(-sign * logit)).astype(BF16)


def sign_of(a, b):
    return jnp.where(a == b, 1.0, -1.0)


def swap_matrix():
    order = np.arange(8 * PIECE).reshape(8, 8, SLOTS).transpose(1, 0, 2).reshape(-1)
    return np.eye(8 * PIECE, dtype=np.float32)[order].astype(jnp.bfloat16)


def half_matrix():
    order = np.arange(2 * BLOCK).reshape(PLANE, 2, SLOTS).transpose(1, 0, 2).reshape(-1)
    return np.eye(2 * BLOCK, dtype=np.float32)[order].astype(jnp.bfloat16)


def route_kernel(tokens, routes, quota, packed, position):
    half = packed.shape[1]
    ids = as_column(routes[...].astype(F32)).astype(jnp.int32)
    hit = ids == iota((TOK, EXPERTS), 1)
    onehot = jnp.where(hit, 1.0, 0.0)
    before = dot(
        jnp.where(iota((TOK, TOK), 1) < iota((TOK, TOK), 0), 1.0, 0.0).astype(BF16),
        onehot.astype(BF16),
    )
    slot = jnp.sum(onehot * before, axis=1, keepdims=True)
    limit = jnp.sum(onehot * quota[...].astype(F32), axis=1, keepdims=True)
    kept = slot < limit
    far = jnp.where(ids >= PLANE, 1, 0)
    place = (ids - far * PLANE) * (2 * SLOTS) + far * SLOTS
    column = jnp.where(kept, place.astype(F32) + slot, -1.0)
    placing = as_row(column)
    position[...] = placing
    id_row = as_row(ids.astype(F32))
    slot_row = as_row(jnp.where(kept, slot, 64.0))
    line = iota((16, TOK), 0)
    packed[0:TOK, :] = tokens[...]
    packed[TOK:ROWS, :] = jnp.zeros((16, half), BF16)
    packed[TOK:ROWS, 0:TOK] = jnp.where(
        line == 0, id_row, jnp.where(line == 1, slot_row, 0.0)
    ).astype(BF16)


def dispatch_kernel(tokens, position, outgoing):
    place = position[...].astype(jnp.int32)
    onto = jnp.where(iota((EXPERTS * SLOTS, TOK), 0) == place, 1.0, 0.0).astype(BF16)
    outgoing[...] = dot(onto, tokens[...]).astype(BF16)


def dispatch(tokens, position, half):
    return pl.pallas_call(
        dispatch_kernel,
        grid=(1,),
        out_shape=struct((EXPERTS * SLOTS, half), BF16),
        in_specs=[part((TOK, half), (0, 1)), whole((1, TOK))],
        out_specs=whole((EXPERTS * SLOTS, half)),
        cost_estimate=pl.CostEstimate(flops=1 << 28, bytes_accessed=1 << 20, transcendentals=0),
        compiler_params=pltpu.CompilerParams(vmem_limit_bytes=60 << 20),
    )(tokens, position)


def route(tokens, routes, quota, half):
    return pl.pallas_call(
        route_kernel,
        grid=(1,),
        out_shape=(struct((ROWS, half), BF16), struct((1, TOK), F32)),
        in_specs=[part((TOK, half), (0, 0)), whole((1, TOK)), whole((1, EXPERTS))],
        out_specs=(whole((ROWS, half)), whole((1, TOK))),
        cost_estimate=pl.CostEstimate(flops=1 << 24, bytes_accessed=1 << 20, transcendentals=0),
        compiler_params=pltpu.CompilerParams(vmem_limit_bytes=60 << 20),
    )(tokens, routes, quota)


def choose_kernel(gathered, side, swap, chosen, target, held):
    first = side[0, 0].astype(F32) * PLANE
    for z in range(RING):
        info = gathered[z * ROWS + TOK : (z + 1) * ROWS, 0:TOK].astype(F32)
        ids = info[0:1] - first
        slot = info[1:2]
        mine = (ids >= 0.0) & (ids < float(PLANE)) & (slot < float(SLOTS))
        row = jnp.where(mine, ids * SLOTS + slot, -1.0)
        target[z : z + 1, :] = row
        onto = jnp.where(iota((BLOCK, TOK), 0) == row.astype(jnp.int32), 1.0, 0.0).astype(BF16)
        held[z * BLOCK : (z + 1) * BLOCK, :] = dot(
            onto, gathered[z * ROWS : z * ROWS + TOK, :]
        ).astype(BF16)
    for g in range(GROUPS):
        rows = jnp.concatenate(
            [held[z * BLOCK + g * PIECE : z * BLOCK + (g + 1) * PIECE, :] for z in range(RING)], 0
        )
        chosen[g * 8 * PIECE : (g + 1) * 8 * PIECE, :] = dot(swap[...], rows).astype(BF16)


def spread_kernel(rows, swap, out):
    for g in range(GROUPS):
        moved = dot(swap[...], rows[g * 8 * PIECE : (g + 1) * 8 * PIECE, :]).astype(BF16)
        for z in range(RING):
            at = z * BLOCK + g * PIECE
            out[at : at + PIECE, :] = moved[z * PIECE : (z + 1) * PIECE, :]


def unspread_kernel(rows, swap, out):
    for g in range(GROUPS):
        starts = [z * BLOCK + g * PIECE for z in range(RING)]
        piece = jnp.concatenate([rows[at : at + PIECE, :] for at in starts], 0)
        out[g * 8 * PIECE : (g + 1) * 8 * PIECE, :] = dot(swap[...], piece).astype(BF16)


def turn_kernel(rows, matrix, out):
    out[...] = dot(matrix[...], rows[...]).astype(BF16)


def expert_kernel(side, rows, partial, first, second, hidden, term):
    x = jnp.concatenate([rows[0, 0], rows[1, 0]], 0)
    value = jax.nn.gelu(partial[...] + dot(x, first[...])).astype(BF16)
    hidden[...] = value
    result = dot_t(value, second[...]).astype(BF16)
    nothing = jnp.zeros((BLOCK, result.shape[1]), BF16)
    for k in range(2):
        mine = result[k * BLOCK : (k + 1) * BLOCK]
        for far in range(2):
            term[k, far] = jnp.where(side[0] == far, mine, nothing)


def expert_right(side, rows, partial, first, second):
    half, inner = rows.shape[3], first.shape[1]
    spec = pl.BlockSpec
    return pl.pallas_call(
        expert_kernel,
        out_shape=(
            struct((RING * BLOCK, inner), BF16),
            struct((RING, 2, BLOCK, half), BF16),
        ),
        grid_spec=pltpu.PrefetchScalarGridSpec(
            num_scalar_prefetch=1,
            grid=(RING // 2,),
            in_specs=[
                spec((2, 1, BLOCK, half), lambda i, side: (i, side[0], 0, 0)),
                spec((2 * BLOCK, inner), lambda i, side: (i, 0)),
                spec((half, inner), lambda i, side: (1, 0)),
                spec((half, inner), lambda i, side: (1, 0)),
            ],
            out_specs=[
                spec((2 * BLOCK, inner), lambda i, side: (i, 0)),
                spec((2, 2, BLOCK, half), lambda i, side: (i, 0, 0, 0)),
            ],
        ),
        cost_estimate=pl.CostEstimate(
            flops=4 * RING * BLOCK * half * inner, bytes_accessed=20 << 20, transcendentals=0
        ),
        compiler_params=pltpu.CompilerParams(vmem_limit_bytes=60 << 20),
    )(side, rows, partial, first, second)


def scatter_kernel(rows, swap, target, out, held):
    for g in range(GROUPS):
        moved = dot(swap[...], rows[g * 8 * PIECE : (g + 1) * 8 * PIECE, :]).astype(BF16)
        for z in range(RING):
            at = z * BLOCK + g * PIECE
            held[at : at + PIECE, :] = moved[z * PIECE : (z + 1) * PIECE, :]
    for z in range(RING):
        column = as_column(target[z : z + 1, :]).astype(jnp.int32)
        onto = jnp.where(iota((TOK, BLOCK), 1) == column, 1.0, 0.0).astype(BF16)
        out[z * TOK : (z + 1) * TOK, :] = dot(
            onto, held[z * BLOCK : (z + 1) * BLOCK, :]
        ).astype(BF16)


def own_rows(layer):
    own = (jnp.sum(layer, axis=0, keepdims=True) / PATCHES).astype(BF16)
    return jnp.broadcast_to(own.astype(F32), (16, layer.shape[1])).astype(BF16)


def right_kernel(tokens, position, gate, returned, head, layer_out, image):
    column = as_column(position[...]).astype(jnp.int32)
    onto = jnp.where(iota((TOK, EXPERTS * SLOTS), 1) == column, 1.0, 0.0).astype(BF16)
    weight = as_column(gate[...])
    layer = tokens[...].astype(F32) + weight * dot(onto, returned[...])
    layer_out[...] = layer.astype(BF16)
    image[...] = dot(own_rows(layer), head[...])


def left_kernel(tokens, gate, given, head, partial, label, other_half, layer_out, own_image):
    layer = tokens[...].astype(F32) + as_column(gate[...]) * given[...].astype(F32)
    layer_out[...] = layer.astype(BF16)
    image = normalize_rows(partial[...] + dot(own_rows(layer), head[...]))[0:1]
    embed = image.shape[1]
    own_image[:, :embed] = image.astype(BF16)
    own_image[:, embed:] = label[:, 0:128].astype(F32).astype(BF16)


def whole(shape):
    return pl.BlockSpec(shape, lambda i: (0,) * len(shape))


def part(shape, at):
    return pl.BlockSpec(shape, lambda i: at)


def layer_right(tokens, position, gate, returned, head):
    half, embed = returned.shape[1], head.shape[1]
    return pl.pallas_call(
        right_kernel,
        grid=(1,),
        out_shape=(struct(tokens.shape, BF16), struct((16, embed), F32)),
        in_specs=[
            part((TOK, half), (0, 1)),
            whole((1, TOK)),
            whole((1, TOK)),
            whole(returned.shape),
            part((half, embed), (1, 0)),
        ],
        out_specs=(part((TOK, half), (0, 1)), whole((16, embed))),
        cost_estimate=pl.CostEstimate(flops=1 << 28, bytes_accessed=4 << 20, transcendentals=0),
        compiler_params=pltpu.CompilerParams(vmem_limit_bytes=60 << 20),
    )(tokens, position, gate, returned, head)


def layer_left(tokens, gate, given, head, partial, label, right_done):
    half, embed = given.shape[1], head.shape[1]
    return pl.pallas_call(
        left_kernel,
        grid=(1,),
        out_shape=(struct(tokens.shape, BF16), struct((1, embed + 128), BF16)),
        in_specs=[
            part((TOK, half), (0, 0)),
            whole((1, TOK)),
            whole(given.shape),
            part((half, embed), (0, 0)),
            whole((16, embed)),
            whole(label.shape),
            pl.BlockSpec(memory_space=pl.ANY),
        ],
        out_specs=(part((TOK, half), (0, 0)), whole((1, embed + 128))),
        input_output_aliases={6: 0},
        cost_estimate=pl.CostEstimate(flops=1 << 28, bytes_accessed=4 << 20, transcendentals=0),
        compiler_params=pltpu.CompilerParams(vmem_limit_bytes=60 << 20),
    )(tokens, gate, given, head, partial, label, right_done)


def pack_kernel(pooled, head, text_embed, labels, packed):
    packed[0:PAIRS, :] = normalize_rows(text_embed[...].astype(F32)).astype(BF16)
    image = pltpu.roll(normalize_rows(dot(pooled[...], head[...])), 1, 0)
    image = jnp.where(iota(image.shape, 0) == 0, 0.0, image)
    packed[PAIRS : 2 * PAIRS, :] = image.astype(BF16)
    packed[2 * PAIRS : SHARD, :] = jnp.zeros((16, packed.shape[1]), BF16)
    packed[2 * PAIRS : SHARD, 0:PAIRS] = jnp.where(
        iota((16, PAIRS), 0) == 0, labels[...].astype(F32), 0.0
    ).astype(BF16)


def pack_pairs(pooled, head, text_embed, labels):
    width, embed = head.shape
    return pl.pallas_call(
        pack_kernel,
        grid=(1,),
        out_shape=struct((SHARD, embed), BF16),
        in_specs=[
            whole((PAIRS, width)),
            whole(head.shape),
            whole(text_embed.shape),
            whole(labels.shape),
        ],
        out_specs=whole((SHARD, embed)),
        cost_estimate=pl.CostEstimate(flops=1 << 28, bytes_accessed=4 << 20, transcendentals=0),
        compiler_params=pltpu.CompilerParams(vmem_limit_bytes=60 << 20),
    )(pooled, head, text_embed, labels)


def label_row(shard):
    return shard[2 * PAIRS : SHARD, 0:PAIRS].astype(F32)[0:1]


def score_kernel(own, s1, s2, s3, loss, image_acc, text_acc):
    text = own[0:PAIRS, :]
    image = own[PAIRS : 2 * PAIRS, :]
    mine = as_column(label_row(own))
    losses = jnp.zeros((PAIRS, 1), F32)
    for k, shard in enumerate((own, s1, s2, s3)):
        their_text = shard[0:PAIRS, :]
        their_image = shard[PAIRS : 2 * PAIRS, :]
        sign = sign_of(mine, label_row(shard))
        logit = scale_logit * dot_t(image, their_text) + shift_logit
        losses = losses + jnp.sum(softplus(-sign * logit), axis=1, keepdims=True)
        grad = dot(coefficients(logit, sign), their_text)
        logit = scale_logit * dot_t(text, their_image) + shift_logit
        text_grad = dot(coefficients(logit, sign), their_image)
        image_acc[...] = grad if k == 0 else image_acc[...] + grad
        text_acc[...] = text_grad if k == 0 else text_acc[...] + text_grad
    loss[...] = as_row(losses)


def own_row_kernel(own_image, own, s1, s2, s3, loss, image_acc, loss_out, image_out):
    embed = own.shape[1]
    row = jnp.broadcast_to(own_image[:, :embed].astype(F32), (16, embed)).astype(BF16)
    label = label_row(own)[0:1, 0:1]
    total = jnp.zeros((16, 1), F32)
    grad = jnp.zeros((16, embed), F32)
    for shard in (own, s1, s2, s3):
        their_text = shard[0:PAIRS, :]
        sign = sign_of(label, label_row(shard))
        logit = scale_logit * dot_t(row, their_text) + shift_logit
        total = total + jnp.sum(softplus(-sign * logit), axis=1, keepdims=True)
        grad = grad + dot(coefficients(logit, sign), their_text)
    loss_out[...] = jnp.where(iota((1, PAIRS), 1) == 0, total[0:1], loss[...])
    image_out[...] = image_acc[...]
    image_out[0:1, :] = grad[0:1]


def own_text_kernel(i0, i1, i2, i3, own, text_acc, out):
    embed = own.shape[1]
    line = iota((16, embed), 0)
    place = iota((1, 16), 1)
    images = jnp.zeros((16, embed), F32)
    labels = jnp.full((1, 16), -1.0, F32)
    for k, row in enumerate((i0, i1, i2, i3)):
        images = jnp.where(line == k, row[:, :embed].astype(F32), images)
        labels = jnp.where(place == k, row[:, embed:].astype(F32)[:, 0:1], labels)
    images = images.astype(BF16)
    sign = sign_of(as_column(label_row(own)), labels)
    logit = scale_logit * dot_t(own[0:PAIRS, :], images) + shift_logit
    out[...] = text_acc[...] + dot(coefficients(logit, sign), images)


def shards(
    tokens, routes, gate_prob, expert_quota, w_in, w_out, other_pooled, head, text_embed, labels
):
    width = tokens.shape[1]
    half = width // 2
    embed = head.shape[1]
    swap = jnp.asarray(swap_matrix())
    apart = jnp.asarray(half_matrix())
    together = jnp.asarray(half_matrix().T)
    side = lax.axis_index("zh").astype(jnp.int32).reshape(1, 1)

    packed, position = route(
        tokens, routes.reshape(1, TOK), expert_quota.reshape(1, EXPERTS), half
    )
    outgoing = dispatch(tokens, position, half)

    own_pairs = pack_pairs(other_pooled, head, text_embed, labels.reshape(1, PAIRS))
    shift = lambda value, step: lax.ppermute(
        value, "zl", [(i, (i + step) % LOOP) for i in range(LOOP)]
    )


    def both(right_going, left_going, senders, hops):
        return (
            lax.ppermute(right_going, "zl", [(i, i + hops) for i in senders]),
            lax.ppermute(left_going, "zl", [(LOOP - 1 - i, LOOP - 1 - i - hops) for i in senders]),
        )

    around = lax.all_gather(packed, Z, axis=0, tiled=True)
    received = lax.all_to_all(
        outgoing.reshape(PLANE, 2 * SLOTS, half), FLAT, split_axis=0, concat_axis=0, tiled=True
    ).reshape(2 * BLOCK, half)
    received = call(turn_kernel, struct((2 * BLOCK, half), BF16), flops=1 << 28, vmem=24)(
        received, apart
    )
    received, around, own_pairs = lax.optimization_barrier((received, around, own_pairs))
    right = lax.all_gather(received, Z, axis=0, tiled=True)

    chosen, target = call(
        choose_kernel,
        (struct((RING * BLOCK, half), BF16), struct((RING, TOK), F32)),
        scratch=[pltpu.VMEM((RING * BLOCK, half), BF16)],
        flops=1 << 30,
    )(around, side, swap)
    arrived = lax.all_to_all(
        chosen.reshape(PLANE, PIECE, half), FLAT, split_axis=0, concat_axis=0, tiled=True
    ).reshape(RING * BLOCK, half)
    left = call(spread_kernel, struct((RING * BLOCK, half), BF16), flops=1 << 30, vmem=24)(arrived, swap)


    first = w_in[0]
    second = w_out[0]
    partial = dot(left, first[:half])
    partial, own_pairs = lax.optimization_barrier((partial, own_pairs))
    r1, l1 = both(own_pairs, own_pairs, (0, 1, 2), 1)
    hidden, term_right = expert_right(
        side.reshape(1), right.reshape(RING, 2, BLOCK, half), partial, first, second
    )
    hidden, term_right, r1, l1 = lax.optimization_barrier((hidden, term_right, r1, l1))
    r2, l2 = both(r1, l1, (1, 2), 1)
    result = lax.psum_scatter(
        term_right.reshape(2 * RING * BLOCK, half), Z, scatter_dimension=0, tiled=True
    )
    term_left = lax.optimization_barrier(dot_t(hidden, second[:half]).astype(BF16))
    leaving = call(unspread_kernel, struct((RING * BLOCK, half), BF16), flops=1 << 30, vmem=24)(
        term_left, swap
    )
    leaving, r2, l2 = lax.optimization_barrier((leaving, r2, l2))
    back = lax.all_to_all(
        leaving.reshape(PLANE, PIECE, half), FLAT, split_axis=0, concat_axis=0, tiled=True
    ).reshape(RING * BLOCK, half)
    by_token = call(
        scatter_kernel,
        struct((RING * TOK, half), BF16),
        scratch=[pltpu.VMEM((RING * BLOCK, half), BF16)],
        flops=1 << 30,
    )(back, swap, target)
    by_token, result, own_pairs = lax.optimization_barrier((by_token, result, own_pairs))
    r3, l3 = both(own_pairs, own_pairs, (0,), 3)
    given = lax.psum_scatter(by_token, Z, scatter_dimension=0, tiled=True)
    result = call(turn_kernel, struct((2 * BLOCK, half), BF16), flops=1 << 28, vmem=24)(result, together)
    returned = lax.all_to_all(
        result.reshape(PLANE, 2 * SLOTS, half), FLAT, split_axis=0, concat_axis=0, tiled=True
    ).reshape(2 * BLOCK, half)

    returned, r3, l3 = lax.optimization_barrier((returned, r3, l3))

    square = struct((PAIRS, embed), F32)
    line = struct((1, PAIRS), F32)
    at = lax.axis_index("zl")
    pairs = [
        own_pairs,
        jnp.where(at == 0, l3, r1),
        jnp.where(at <= 1, l2, r2),
        jnp.where(at == 3, r3, l1),
    ]
    loss, image_acc, text_acc = call(score_kernel, (line, square, square), flops=1 << 30)(*pairs)
    gate = gate_prob.reshape(1, TOK)
    layer_out, image_right = layer_right(tokens, position, gate, returned, head)
    loss, image_acc, text_acc, layer_out, image_right, given = lax.optimization_barrier(
        (loss, image_acc, text_acc, layer_out, image_right, given)
    )
    layer_out, own_image = layer_left(
        tokens, gate, given, head, image_right, labels.reshape(1, PAIRS), layer_out
    )
    own_images = [own_image] + [shift(own_image, step) for step in range(1, LOOP)]
    loss, image_acc = call(own_row_kernel, (line, square), flops=1 << 26, vmem=24)(
        own_image, *pairs, loss, image_acc
    )
    text_acc = call(own_text_kernel, square, flops=1 << 26, vmem=24)(*own_images, own_pairs, text_acc)
    return (layer_out, loss.reshape(PAIRS), image_acc, text_acc)


def solution(mesh):
    fine = Mesh(mesh.devices.reshape(2, 4, 4, 2, LOOP), AXES)
    rows = P(AXES, None)
    flat = P(AXES)
    weights = P(EXPERT, None, "zl")
    in_specs = (rows, rows, flat, P(), weights, weights, rows, P(), rows, flat)
    out_specs = (rows, flat, rows, rows)
    return jax.shard_map(shards, mesh=fine, in_specs=in_specs, out_specs=out_specs, check_vma=False)
```

```python
import functools

import jax
import jax.numpy as jnp
import numpy as np
from jax import lax
from jax.experimental import pallas as pl
from jax.experimental.pallas import tpu as pltpu
from jax.sharding import Mesh
from jax.sharding import PartitionSpec as P

PATCHES = 256
PAIRS = 128
LOOP = 4
RING = 8
PLANE = 32
SLOTS = 6
EXPERTS = 64
GROUPS = 4
PIECE = 48
BLOCK = PLANE * SLOTS
TOK = 256
ROWS = TOK + 16
SHARD = 2 * PAIRS + 16

AXES = ("zh", "y", "x", "c", "zl")
EXPERT = ("zh", "y", "x", "c")
FLAT = ("y", "x", "c")
Z = ("zh", "zl")

scale_logit = 4.0
shift_logit = -1.0

F32 = jnp.float32
BF16 = jnp.bfloat16


def call(kernel, out_shape, scratch=(), aliases=None, flops=0, vmem=60):
    return pl.pallas_call(
        kernel,
        out_shape=out_shape,
        scratch_shapes=list(scratch),
        input_output_aliases=aliases or {},
        cost_estimate=pl.CostEstimate(flops=flops, bytes_accessed=4 << 20, transcendentals=0),
        compiler_params=pltpu.CompilerParams(vmem_limit_bytes=vmem << 20),
    )


def struct(shape, dtype):
    return jax.ShapeDtypeStruct(shape, dtype)


def iota(shape, dim):
    return lax.broadcasted_iota(jnp.int32, shape, dim)


def dot(a, b):
    return jnp.dot(a, b, preferred_element_type=F32)


def dot_t(a, b):
    return lax.dot_general(a, b, (((1,), (1,)), ((), ())), preferred_element_type=F32)


def as_row(column):
    n = column.shape[0]
    return jnp.sum(jnp.where(iota((n, n), 0) == iota((n, n), 1), column, 0.0), 0, keepdims=True)


def as_column(row):
    n = row.shape[1]
    return jnp.sum(jnp.where(iota((n, n), 0) == iota((n, n), 1), row, 0.0), 1, keepdims=True)


def normalize_rows(values):
    return values / jnp.sqrt(jnp.sum(values * values, axis=1, keepdims=True) + 1e-06)


def softplus(x):
    return jnp.maximum(x, 0.0) + jnp.log1p(jnp.exp(-jnp.abs(x)))


def coefficients(logit, sign):
    return (-scale_logit * sign * lax.logistic(-sign * logit)).astype(BF16)


def sign_of(a, b):
    return jnp.where(a == b, 1.0, -1.0)


def swap_matrix():
    order = np.arange(8 * PIECE).reshape(8, 8, SLOTS).transpose(1, 0, 2).reshape(-1)
    return np.eye(8 * PIECE, dtype=np.float32)[order].astype(jnp.bfloat16)


def half_matrix():
    order = np.arange(2 * BLOCK).reshape(PLANE, 2, SLOTS).transpose(1, 0, 2).reshape(-1)
    return np.eye(2 * BLOCK, dtype=np.float32)[order].astype(jnp.bfloat16)


def route_kernel(tokens, routes, quota, packed, position):
    half = packed.shape[1]
    ids = as_column(routes[...].astype(F32)).astype(jnp.int32)
    hit = ids == iota((TOK, EXPERTS), 1)
    onehot = jnp.where(hit, 1.0, 0.0)
    before = dot(
        jnp.where(iota((TOK, TOK), 1) < iota((TOK, TOK), 0), 1.0, 0.0).astype(BF16),
        onehot.astype(BF16),
    )
    slot = jnp.sum(onehot * before, axis=1, keepdims=True)
    limit = jnp.sum(onehot * quota[...].astype(F32), axis=1, keepdims=True)
    kept = slot < limit
    far = jnp.where(ids >= PLANE, 1, 0)
    place = (ids - far * PLANE) * (2 * SLOTS) + far * SLOTS
    column = jnp.where(kept, place.astype(F32) + slot, -1.0)
    placing = as_row(column)
    position[...] = placing
    id_row = as_row(ids.astype(F32))
    slot_row = as_row(jnp.where(kept, slot, 64.0))
    line = iota((16, TOK), 0)
    packed[0:TOK, :] = tokens[...]
    packed[TOK:ROWS, :] = jnp.zeros((16, half), BF16)
    packed[TOK:ROWS, 0:TOK] = jnp.where(
        line == 0, id_row, jnp.where(line == 1, slot_row, 0.0)
    ).astype(BF16)


def dispatch_kernel(tokens, position, outgoing):
    place = position[...].astype(jnp.int32)
    onto = jnp.where(iota((EXPERTS * SLOTS, TOK), 0) == place, 1.0, 0.0).astype(BF16)
    outgoing[...] = dot(onto, tokens[...]).astype(BF16)


def dispatch(tokens, position, half):
    return pl.pallas_call(
        dispatch_kernel,
        grid=(1,),
        out_shape=struct((EXPERTS * SLOTS, half), BF16),
        in_specs=[part((TOK, half), (0, 1)), whole((1, TOK))],
        out_specs=whole((EXPERTS * SLOTS, half)),
        cost_estimate=pl.CostEstimate(flops=1 << 28, bytes_accessed=1 << 20, transcendentals=0),
        compiler_params=pltpu.CompilerParams(vmem_limit_bytes=60 << 20),
    )(tokens, position)


def route(tokens, routes, quota, half):
    return pl.pallas_call(
        route_kernel,
        grid=(1,),
        out_shape=(struct((ROWS, half), BF16), struct((1, TOK), F32)),
        in_specs=[part((TOK, half), (0, 0)), whole((1, TOK)), whole((1, EXPERTS))],
        out_specs=(whole((ROWS, half)), whole((1, TOK))),
        cost_estimate=pl.CostEstimate(flops=1 << 24, bytes_accessed=1 << 20, transcendentals=0),
        compiler_params=pltpu.CompilerParams(vmem_limit_bytes=60 << 20),
    )(tokens, routes, quota)


def choose_kernel(gathered, side, swap, chosen, target, held):
    first = side[0, 0].astype(F32) * PLANE
    for z in range(RING):
        info = gathered[z * ROWS + TOK : (z + 1) * ROWS, 0:TOK].astype(F32)
        ids = info[0:1] - first
        slot = info[1:2]
        mine = (ids >= 0.0) & (ids < float(PLANE)) & (slot < float(SLOTS))
        row = jnp.where(mine, ids * SLOTS + slot, -1.0)
        target[z : z + 1, :] = row
        onto = jnp.where(iota((BLOCK, TOK), 0) == row.astype(jnp.int32), 1.0, 0.0).astype(BF16)
        held[z * BLOCK : (z + 1) * BLOCK, :] = dot(
            onto, gathered[z * ROWS : z * ROWS + TOK, :]
        ).astype(BF16)
    for g in range(GROUPS):
        rows = jnp.concatenate(
            [held[z * BLOCK + g * PIECE : z * BLOCK + (g + 1) * PIECE, :] for z in range(RING)], 0
        )
        chosen[g * 8 * PIECE : (g + 1) * 8 * PIECE, :] = dot(swap[...], rows).astype(BF16)


def spread_kernel(rows, swap, out):
    for g in range(GROUPS):
        moved = dot(swap[...], rows[g * 8 * PIECE : (g + 1) * 8 * PIECE, :]).astype(BF16)
        for z in range(RING):
            at = z * BLOCK + g * PIECE
            out[at : at + PIECE, :] = moved[z * PIECE : (z + 1) * PIECE, :]


def unspread_kernel(rows, swap, out):
    for g in range(GROUPS):
        starts = [z * BLOCK + g * PIECE for z in range(RING)]
        piece = jnp.concatenate([rows[at : at + PIECE, :] for at in starts], 0)
        out[g * 8 * PIECE : (g + 1) * 8 * PIECE, :] = dot(swap[...], piece).astype(BF16)


def turn_kernel(rows, matrix, out):
    out[...] = dot(matrix[...], rows[...]).astype(BF16)


def expert_kernel(side, rows, partial, first, second, hidden, term):
    x = jnp.concatenate([rows[0, 0], rows[1, 0]], 0)
    value = jax.nn.gelu(partial[...] + dot(x, first[...])).astype(BF16)
    hidden[...] = value
    result = dot_t(value, second[...]).astype(BF16)
    nothing = jnp.zeros((BLOCK, result.shape[1]), BF16)
    for k in range(2):
        mine = result[k * BLOCK : (k + 1) * BLOCK]
        for far in range(2):
            term[k, far] = jnp.where(side[0] == far, mine, nothing)


def expert_right(side, rows, partial, first, second):
    half, inner = rows.shape[3], first.shape[1]
    spec = pl.BlockSpec
    return pl.pallas_call(
        expert_kernel,
        out_shape=(
            struct((RING * BLOCK, inner), BF16),
            struct((RING, 2, BLOCK, half), BF16),
        ),
        grid_spec=pltpu.PrefetchScalarGridSpec(
            num_scalar_prefetch=1,
            grid=(RING // 2,),
            in_specs=[
                spec((2, 1, BLOCK, half), lambda i, side: (i, side[0], 0, 0)),
                spec((2 * BLOCK, inner), lambda i, side: (i, 0)),
                spec((half, inner), lambda i, side: (1, 0)),
                spec((half, inner), lambda i, side: (1, 0)),
            ],
            out_specs=[
                spec((2 * BLOCK, inner), lambda i, side: (i, 0)),
                spec((2, 2, BLOCK, half), lambda i, side: (i, 0, 0, 0)),
            ],
        ),
        cost_estimate=pl.CostEstimate(
            flops=4 * RING * BLOCK * half * inner, bytes_accessed=20 << 20, transcendentals=0
        ),
        compiler_params=pltpu.CompilerParams(vmem_limit_bytes=60 << 20),
    )(side, rows, partial, first, second)


def scatter_kernel(rows, swap, target, out, held):
    for g in range(GROUPS):
        moved = dot(swap[...], rows[g * 8 * PIECE : (g + 1) * 8 * PIECE, :]).astype(BF16)
        for z in range(RING):
            at = z * BLOCK + g * PIECE
            held[at : at + PIECE, :] = moved[z * PIECE : (z + 1) * PIECE, :]
    for z in range(RING):
        column = as_column(target[z : z + 1, :]).astype(jnp.int32)
        onto = jnp.where(iota((TOK, BLOCK), 1) == column, 1.0, 0.0).astype(BF16)
        out[z * TOK : (z + 1) * TOK, :] = dot(
            onto, held[z * BLOCK : (z + 1) * BLOCK, :]
        ).astype(BF16)


def own_rows(layer):
    own = (jnp.sum(layer, axis=0, keepdims=True) / PATCHES).astype(BF16)
    return jnp.broadcast_to(own.astype(F32), (16, layer.shape[1])).astype(BF16)


def right_kernel(tokens, position, gate, returned, head, layer_out, image):
    column = as_column(position[...]).astype(jnp.int32)
    onto = jnp.where(iota((TOK, EXPERTS * SLOTS), 1) == column, 1.0, 0.0).astype(BF16)
    weight = as_column(gate[...])
    layer = tokens[...].astype(F32) + weight * dot(onto, returned[...])
    layer_out[...] = layer.astype(BF16)
    image[...] = dot(own_rows(layer), head[...])


def left_kernel(tokens, gate, given, head, partial, label, other_half, layer_out, own_image):
    layer = tokens[...].astype(F32) + as_column(gate[...]) * given[...].astype(F32)
    layer_out[...] = layer.astype(BF16)
    image = normalize_rows(partial[...] + dot(own_rows(layer), head[...]))[0:1]
    embed = image.shape[1]
    own_image[:, :embed] = image.astype(BF16)
    own_image[:, embed:] = label[:, 0:128].astype(F32).astype(BF16)


def whole(shape):
    return pl.BlockSpec(shape, lambda i: (0,) * len(shape))


def part(shape, at):
    return pl.BlockSpec(shape, lambda i: at)


def layer_right(tokens, position, gate, returned, head):
    half, embed = returned.shape[1], head.shape[1]
    return pl.pallas_call(
        right_kernel,
        grid=(1,),
        out_shape=(struct(tokens.shape, BF16), struct((16, embed), F32)),
        in_specs=[
            part((TOK, half), (0, 1)),
            whole((1, TOK)),
            whole((1, TOK)),
            whole(returned.shape),
            part((half, embed), (1, 0)),
        ],
        out_specs=(part((TOK, half), (0, 1)), whole((16, embed))),
        cost_estimate=pl.CostEstimate(flops=1 << 28, bytes_accessed=4 << 20, transcendentals=0),
        compiler_params=pltpu.CompilerParams(vmem_limit_bytes=60 << 20),
    )(tokens, position, gate, returned, head)


def layer_left(tokens, gate, given, head, partial, label, right_done):
    half, embed = given.shape[1], head.shape[1]
    return pl.pallas_call(
        left_kernel,
        grid=(1,),
        out_shape=(struct(tokens.shape, BF16), struct((1, embed + 128), BF16)),
        in_specs=[
            part((TOK, half), (0, 0)),
            whole((1, TOK)),
            whole(given.shape),
            part((half, embed), (0, 0)),
            whole((16, embed)),
            whole(label.shape),
            pl.BlockSpec(memory_space=pl.ANY),
        ],
        out_specs=(part((TOK, half), (0, 0)), whole((1, embed + 128))),
        input_output_aliases={6: 0},
        cost_estimate=pl.CostEstimate(flops=1 << 28, bytes_accessed=4 << 20, transcendentals=0),
        compiler_params=pltpu.CompilerParams(vmem_limit_bytes=60 << 20),
    )(tokens, gate, given, head, partial, label, right_done)


def pack_kernel(pooled, head, text_embed, labels, packed):
    packed[0:PAIRS, :] = normalize_rows(text_embed[...].astype(F32)).astype(BF16)
    image = pltpu.roll(normalize_rows(dot(pooled[...], head[...])), 1, 0)
    image = jnp.where(iota(image.shape, 0) == 0, 0.0, image)
    packed[PAIRS : 2 * PAIRS, :] = image.astype(BF16)
    packed[2 * PAIRS : SHARD, :] = jnp.zeros((16, packed.shape[1]), BF16)
    packed[2 * PAIRS : SHARD, 0:PAIRS] = jnp.where(
        iota((16, PAIRS), 0) == 0, labels[...].astype(F32), 0.0
    ).astype(BF16)


def pack_pairs(pooled, head, text_embed, labels):
    width, embed = head.shape
    return pl.pallas_call(
        pack_kernel,
        grid=(1,),
        out_shape=struct((SHARD, embed), BF16),
        in_specs=[
            whole((PAIRS, width)),
            whole(head.shape),
            whole(text_embed.shape),
            whole(labels.shape),
        ],
        out_specs=whole((SHARD, embed)),
        cost_estimate=pl.CostEstimate(flops=1 << 28, bytes_accessed=4 << 20, transcendentals=0),
        compiler_params=pltpu.CompilerParams(vmem_limit_bytes=60 << 20),
    )(pooled, head, text_embed, labels)


def label_row(shard):
    return shard[2 * PAIRS : SHARD, 0:PAIRS].astype(F32)[0:1]


def score_kernel(own, s1, s2, s3, loss, image_acc, text_acc):
    text = own[0:PAIRS, :]
    image = own[PAIRS : 2 * PAIRS, :]
    mine = as_column(label_row(own))
    losses = jnp.zeros((PAIRS, 1), F32)
    for k, shard in enumerate((own, s1, s2, s3)):
        their_text = shard[0:PAIRS, :]
        their_image = shard[PAIRS : 2 * PAIRS, :]
        sign = sign_of(mine, label_row(shard))
        logit = scale_logit * dot_t(image, their_text) + shift_logit
        losses = losses + jnp.sum(softplus(-sign * logit), axis=1, keepdims=True)
        grad = dot(coefficients(logit, sign), their_text)
        logit = scale_logit * dot_t(text, their_image) + shift_logit
        text_grad = dot(coefficients(logit, sign), their_image)
        image_acc[...] = grad if k == 0 else image_acc[...] + grad
        text_acc[...] = text_grad if k == 0 else text_acc[...] + text_grad
    loss[...] = as_row(losses)


def own_row_kernel(own_image, own, s1, s2, s3, loss, image_acc, loss_out, image_out):
    embed = own.shape[1]
    row = jnp.broadcast_to(own_image[:, :embed].astype(F32), (16, embed)).astype(BF16)
    label = label_row(own)[0:1, 0:1]
    total = jnp.zeros((16, 1), F32)
    grad = jnp.zeros((16, embed), F32)
    for shard in (own, s1, s2, s3):
        their_text = shard[0:PAIRS, :]
        sign = sign_of(label, label_row(shard))
        logit = scale_logit * dot_t(row, their_text) + shift_logit
        total = total + jnp.sum(softplus(-sign * logit), axis=1, keepdims=True)
        grad = grad + dot(coefficients(logit, sign), their_text)
    loss_out[...] = jnp.where(iota((1, PAIRS), 1) == 0, total[0:1], loss[...])
    image_out[...] = image_acc[...]
    image_out[0:1, :] = grad[0:1]


def own_text_kernel(i0, i1, i2, i3, own, text_acc, out):
    embed = own.shape[1]
    line = iota((16, embed), 0)
    place = iota((1, 16), 1)
    images = jnp.zeros((16, embed), F32)
    labels = jnp.full((1, 16), -1.0, F32)
    for k, row in enumerate((i0, i1, i2, i3)):
        images = jnp.where(line == k, row[:, :embed].astype(F32), images)
        labels = jnp.where(place == k, row[:, embed:].astype(F32)[:, 0:1], labels)
    images = images.astype(BF16)
    sign = sign_of(as_column(label_row(own)), labels)
    logit = scale_logit * dot_t(own[0:PAIRS, :], images) + shift_logit
    out[...] = text_acc[...] + dot(coefficients(logit, sign), images)


def shards(
    tokens, routes, gate_prob, expert_quota, w_in, w_out, other_pooled, head, text_embed, labels
):
    width = tokens.shape[1]
    half = width // 2
    embed = head.shape[1]
    swap = jnp.asarray(swap_matrix())
    apart = jnp.asarray(half_matrix())
    together = jnp.asarray(half_matrix().T)
    side = lax.axis_index("zh").astype(jnp.int32).reshape(1, 1)

    packed, position = route(
        tokens, routes.reshape(1, TOK), expert_quota.reshape(1, EXPERTS), half
    )
    outgoing = dispatch(tokens, position, half)

    own_pairs = pack_pairs(other_pooled, head, text_embed, labels.reshape(1, PAIRS))
    shift = lambda value, step: lax.ppermute(
        value, "zl", [(i, (i + step) % LOOP) for i in range(LOOP)]
    )


    def both(right_going, left_going, senders, hops):
        return (
            lax.ppermute(right_going, "zl", [(i, i + hops) for i in senders]),
            lax.ppermute(left_going, "zl", [(LOOP - 1 - i, LOOP - 1 - i - hops) for i in senders]),
        )

    around = lax.all_gather(packed, Z, axis=0, tiled=True)
    received = lax.all_to_all(
        outgoing.reshape(PLANE, 2 * SLOTS, half), FLAT, split_axis=0, concat_axis=0, tiled=True
    ).reshape(2 * BLOCK, half)
    received = call(turn_kernel, struct((2 * BLOCK, half), BF16), flops=1 << 28, vmem=24)(
        received, apart
    )
    received, around, own_pairs = lax.optimization_barrier((received, around, own_pairs))
    right = lax.all_gather(received, Z, axis=0, tiled=True)

    chosen, target = call(
        choose_kernel,
        (struct((RING * BLOCK, half), BF16), struct((RING, TOK), F32)),
        scratch=[pltpu.VMEM((RING * BLOCK, half), BF16)],
        flops=1 << 30,
    )(around, side, swap)
    arrived = lax.all_to_all(
        chosen.reshape(PLANE, PIECE, half), FLAT, split_axis=0, concat_axis=0, tiled=True
    ).reshape(RING * BLOCK, half)
    left = call(spread_kernel, struct((RING * BLOCK, half), BF16), flops=1 << 30, vmem=24)(arrived, swap)


    first = w_in[0]
    second = w_out[0]
    partial = dot(left, first[:half])
    partial, own_pairs = lax.optimization_barrier((partial, own_pairs))
    r1, l1 = both(own_pairs, own_pairs, (0, 1, 2), 1)
    hidden, term_right = expert_right(
        side.reshape(1), right.reshape(RING, 2, BLOCK, half), partial, first, second
    )
    hidden, term_right, r1, l1 = lax.optimization_barrier((hidden, term_right, r1, l1))
    r2, l2 = both(r1, l1, (1, 2), 1)
    result = lax.psum_scatter(
        term_right.reshape(2 * RING * BLOCK, half), Z, scatter_dimension=0, tiled=True
    )
    term_left = lax.optimization_barrier(dot_t(hidden, second[:half]).astype(BF16))
    leaving = call(unspread_kernel, struct((RING * BLOCK, half), BF16), flops=1 << 30, vmem=24)(
        term_left, swap
    )
    leaving, r2, l2 = lax.optimization_barrier((leaving, r2, l2))
    back = lax.all_to_all(
        leaving.reshape(PLANE, PIECE, half), FLAT, split_axis=0, concat_axis=0, tiled=True
    ).reshape(RING * BLOCK, half)
    by_token = call(
        scatter_kernel,
        struct((RING * TOK, half), BF16),
        scratch=[pltpu.VMEM((RING * BLOCK, half), BF16)],
        flops=1 << 30,
    )(back, swap, target)
    by_token, result, r2, l2 = lax.optimization_barrier((by_token, result, r2, l2))
    r3, l3 = both(r2, l2, (2,), 1)
    given = lax.psum_scatter(by_token, Z, scatter_dimension=0, tiled=True)
    result = call(turn_kernel, struct((2 * BLOCK, half), BF16), flops=1 << 28, vmem=24)(result, together)
    returned = lax.all_to_all(
        result.reshape(PLANE, 2 * SLOTS, half), FLAT, split_axis=0, concat_axis=0, tiled=True
    ).reshape(2 * BLOCK, half)

    returned, r3, l3 = lax.optimization_barrier((returned, r3, l3))

    square = struct((PAIRS, embed), F32)
    line = struct((1, PAIRS), F32)
    at = lax.axis_index("zl")
    pairs = [
        own_pairs,
        jnp.where(at == 0, l3, r1),
        jnp.where(at <= 1, l2, r2),
        jnp.where(at == 3, r3, l1),
    ]
    loss, image_acc, text_acc = call(score_kernel, (line, square, square), flops=1 << 30)(*pairs)
    gate = gate_prob.reshape(1, TOK)
    layer_out, image_right = layer_right(tokens, position, gate, returned, head)
    loss, image_acc, text_acc, layer_out, image_right, given = lax.optimization_barrier(
        (loss, image_acc, text_acc, layer_out, image_right, given)
    )
    layer_out, own_image = layer_left(
        tokens, gate, given, head, image_right, labels.reshape(1, PAIRS), layer_out
    )
    own_images = [own_image] + [shift(own_image, step) for step in range(1, LOOP)]
    loss, image_acc = call(own_row_kernel, (line, square), flops=1 << 26, vmem=24)(
        own_image, *pairs, loss, image_acc
    )
    text_acc = call(own_text_kernel, square, flops=1 << 26, vmem=24)(*own_images, own_pairs, text_acc)
    return (layer_out, loss.reshape(PAIRS), image_acc, text_acc)


def solution(mesh):
    fine = Mesh(mesh.devices.reshape(2, 4, 4, 2, LOOP), AXES)
    rows = P(AXES, None)
    flat = P(AXES)
    weights = P(EXPERT, None, "zl")
    in_specs = (rows, rows, flat, P(), weights, weights, rows, P(), rows, flat)
    out_specs = (rows, flat, rows, rows)
    return jax.shard_map(shards, mesh=fine, in_specs=in_specs, out_specs=out_specs, check_vma=False)
```
